256 devices in a mesh: seq: 64 (over y, x_lo, z), filt: 4 (over x_hi, core).
Axes of the slice: x: 4 (x_hi: 2, x_lo: 2; x = x_hi * 2 + x_lo), y: 4, z: 8, core: 2. Of those that a mesh axis runs over, the one named last changes fastest.
Arguments:
- inputs: bfloat16 [8192, 1024], P('seq'), may hold values from -16 to 16
- cotangent: bfloat16 [8192, 1024], P('seq'), may hold values from -6 to 6
- filters: bfloat16 [12, 8192], replicated, may hold values from -0.0625 to 0.0625
- projections: bfloat16 [12, 1024, 1024], P('filt'), may hold values from -0.1875 to 0.1875
Outputs:
- input_grad: bfloat16 [8192, 1024], P('seq', 'filt')
- projection_grad: bfloat16 [12, 1024, 1024], P('filt', 'seq')
The draws below stay inside these ranges and needn't reach their ends.
All inputs are finite; a program needn't handle non-finite values.
Results may differ from the reference program's by a relative error of at most 0.015.
Values may be sent and summed in bfloat16 or wider, within the bound.
A program may use at most 192 MiB of HBM per device.

```python
import jax
import jax.numpy as jnp
from jax import lax

D = 1024
K = 12
L = 8192


def with_spikes(values, own_key, source, target, shards_of, factor):
    owner, partner = [(jnp.arange(values.shape[position]) // (values.shape[position] // shards_of)).reshape([-1 if axis == position else 1 for axis in range(values.ndim)]) for position in (source, target)]
    chosen = jax.random.permutation(own_key, shards_of)[partner]
    strong = (owner == chosen) | (owner == (partner + shards_of // 2) % shards_of)
    return jnp.where(strong, factor * values, values)


def block_levels(key, extent, split, low, largest):
    def one(axis_at, shards_of):
        heights = jax.random.uniform(jax.random.fold_in(jax.random.fold_in(key, 6), axis_at), (shards_of,), jnp.float32, low / len(split), largest / len(split))
        return jnp.repeat(jnp.exp(heights), extent[axis_at] // shards_of).reshape((-1,) + (1,) * (len(extent) - axis_at - 1))

    loudness = one(*split[0])
    for cut in split[1:]:
        loudness = loudness * one(*cut)
    return loudness


def centred(rng, shape, spread, reach, split=(), dtype=jnp.bfloat16):
    loudness = block_levels(rng, shape, split, -0.22, 0.18) if split else 1.0
    drawn = jax.random.normal(rng, shape, jnp.float32) * spread * loudness
    return jnp.minimum(jnp.maximum(drawn, -reach), reach).astype(dtype)


def heavy_noise(rng, shape, deviation, limit, pieces, heavy, kind=jnp.bfloat16):
    result = deviation * jax.random.normal(rng, shape, jnp.float32)
    if pieces:
        result = result * block_levels(rng, shape, pieces, -0.22, 0.18)
    return jnp.clip(with_spikes(result, jax.random.fold_in(rng, 3), *heavy), -limit, limit).astype(kind)


def setup_inputs(seed: int = 0) -> dict:
    splits = jax.random.split(jax.random.key(seed), 5)
    return {
        "inputs": heavy_noise(splits[0], (L, D), 1.0, 16.0, ((0, 64),), (0, 1, 64, 4.0)),
        "cotangent": centred(splits[1], (L, D), 1.0, 6.0, ((0, 64),)),
        "filters": centred(splits[2], (K, L), L ** -0.5, 0.0625),
        "projections": centred(splits[3], (K, D, D), D ** -0.5, 0.1875, ((0, 4),)),
    }


def correlate(taps, cot_wide):
    length = cot_wide.shape[0]
    spectrum = jnp.fft.rfft(cot_wide[::-1], 2 * length, axis=0) * jnp.fft.rfft(taps, 2 * length)[:, None]
    return jnp.fft.irfft(spectrum, 2 * length, axis=0)[:length][::-1]


def reference(inputs, cotangent, filters, projections):
    cot_wide = cotangent.astype(jnp.float32)
    corr = lax.map(lambda taps: correlate(taps.astype(jnp.float32), cot_wide).astype(jnp.bfloat16), filters)
    corr_wide = corr.astype(jnp.float32)
    input_grad = jnp.einsum("ksc,kec->se", corr_wide, projections.astype(jnp.float32), precision=lax.Precision.HIGHEST)
    scale = L ** -0.5
    projection_grad = jnp.einsum("sd,kse->kde", inputs.astype(jnp.float32), corr_wide, precision=lax.Precision.HIGHEST) * scale
    return input_grad.astype(jnp.bfloat16), projection_grad.astype(jnp.bfloat16)
```

```python
import functools

import jax
import jax.numpy as jnp
from jax import lax
from jax.experimental import pallas as pl
from jax.experimental.pallas import tpu as pltpu
from jax.sharding import PartitionSpec as P

MESH = pl.DeviceIdType.MESH
F32 = jnp.float32
BF16 = jnp.bfloat16
B = 128
ORDER = (0, 1, -1, 2, -2, 3, -3, 4)


def kernel(
    x_ref, g_ref, f_ref, p_ref, ig_ref, pg_ref,
    taps, hank, gl, g2, acc, corr, xs, xt, pn, pgb, pgr, pgs, pga, pgo,
    igs, igr, igo, igc, igd,
    ga_s, ga_r, gr_s, gr_r, gs_s, gs_r, xa_s, xa_r, xs_s, xs_r, loc,
    pr_s, pr_r, pa_s, pa_r, is_s, is_r, id_s, id_r,
):
    seq = lax.axis_index("seq")
    filt = lax.axis_index("filt")
    q, z = lax.div(seq, 8), lax.rem(seq, 8)
    xh, core = lax.div(filt, 2), lax.rem(filt, 2)
    sib = (seq, xh * 2 + 1 - core)
    up = (q * 8 + lax.rem(z + 1, 8), filt)
    down = (q * 8 + lax.rem(z + 7, 8), filt)

    def plane(dx, dq):
        return (lax.rem(q + dq, 8) * 8 + z, lax.rem(xh + dx, 2) * 2 + core)

    def remote(src, dst, send, recv, to):
        return pltpu.make_async_remote_copy(
            src_ref=src, dst_ref=dst, send_sem=send, recv_sem=recv,
            device_id=to, device_id_type=MESH,
        )

    sent = []

    def go(copy):
        copy.start()
        sent.append(copy)

    barrier = pltpu.get_barrier_semaphore()
    partners = [sib, up, down] + [plane(r // 8, r % 8) for r in range(1, 16)]
    for to in partners:
        pl.semaphore_signal(barrier, inc=1, device_id=to, device_id_type=MESH)

    p_copies = [
        pltpu.make_async_copy(
            p_ref.at[k, :, pl.ds(pl.multiple_of(q * B, B), B)],
            pn.at[:, pl.ds(k * B, B)],
            loc.at[k],
        )
        for k in range(3)
    ]
    for c in p_copies:
        c.start()
    pick = jnp.where(
        lax.broadcasted_iota(jnp.int32, (8, 12), 1)
        == lax.broadcasted_iota(jnp.int32, (8, 12), 0) + 3 * filt,
        1.0, 0.0,
    ).astype(BF16)
    taps[...] = jnp.dot(pick, f_ref[...], preferred_element_type=F32)
    g2[...] = jnp.zeros_like(g2)
    rows = pl.ds(pl.multiple_of(core * 64, 64), 64)
    gl[0, core, q] = g_ref[rows, pl.ds(pl.multiple_of(q * B, B), B)]

    pl.semaphore_wait(barrier, len(partners))

    a2a = []
    for r in range(1, 8):
        col = pl.ds(pl.multiple_of(lax.rem(q + r, 8) * B, B), B)
        a2a.append(
            remote(g_ref.at[rows, col], gl.at[0, core, q], ga_s.at[r], ga_r.at[r], plane(0, r))
        )
        go(a2a[-1])

    for t in range(8):
        flip = x_ref[:, t * B:(t + 1) * B].T
        for zz in range(8):
            xs[zz, t * 16:(t + 1) * 16, :] = flip[zz * 16:(zz + 1) * 16]
    half = pl.ds(core * 4, 4)
    lanes = pl.ds(pl.multiple_of(q * B, B), B)
    x_own = pltpu.make_async_copy(xs.at[half], xt.at[half, :, lanes], loc.at[3])
    x_own.start()

    upper = lax.broadcasted_iota(jnp.int32, (B, B), 1) >= lax.broadcasted_iota(
        jnp.int32, (B, B), 0
    )
    for k in range(3):
        def build(n, before, k=k):
            row = taps[k:k + 1, pl.ds(pl.multiple_of(n * B, B), B)]
            turned = pltpu.roll(
                jnp.broadcast_to(row, (B, B)), 0, 1, stride=1, stride_axis=0
            )
            block = jnp.where(upper, turned, before)
            hank[lax.rem(n, 8), k * B:(k + 1) * B,
                 pl.ds(pl.multiple_of(lax.div(n, 8) * B, B), B)] = block.astype(BF16)
            return turned

        lax.fori_loop(0, 64, build, jnp.zeros((B, B), F32), unroll=2)

    def sub(slot, s):
        return gl.at[slot, core, pl.ds(s * 4, 4)]

    def ring_send(step, s, way):
        here = -step % 8 if way == 0 else step
        there = (-step - 1) % 8 if way == 0 else step + 1
        return remote(
            sub(here, s), sub(there, s),
            gr_s.at[way, step, s], gr_r.at[way, step, s], up if way == 0 else down,
        )

    def hand_over(slot, s):
        return remote(sub(slot, s), sub(slot, s), gs_s.at[slot, s], gs_r.at[slot, s], sib)

    def handed(slot, s):
        other = gl.at[slot, 1 - core, pl.ds(s * 4, 4)]
        return remote(other, other, gs_s.at[slot, s], gs_r.at[slot, s], sib)

    for c in a2a:
        c.wait_recv()
    for s in range(2):
        for way in range(2):
            go(ring_send(0, s, way))
    for s in range(2):
        go(hand_over(0, s))

    x_sends = []
    for r in range(1, 8):
        x_sends.append(
            remote(xs.at[half], xt.at[half, :, lanes], xa_s.at[r], xa_r.at[r], plane(0, r))
        )
        go(x_sends[-1])

    first = [True]

    def conv(o):
        slot = o % 8
        for s in range(2):
            handed(slot, s).wait_recv()
        buf = g2.at[0]
        for m in range(8):
            for h in range(2):
                piece = gl[slot, h, m]
                buf[m * B + h * 64:m * B + h * 64 + 64, 0:B] = piece
                if m > 0:
                    buf[(m - 1) * B + h * 64:(m - 1) * B + h * 64 + 64, B:2 * B] = piece
        wrap = jnp.where(lax.rem(z + o + 8, 8) < z, 1, 0)
        for p in range(4):
            depth = B * (8 - 2 * p)
            start = pl.multiple_of(wrap * B + 2 * p * B, B)
            term = jnp.dot(
                hank[slot, :, 0:depth], buf[pl.ds(start, depth), :],
                preferred_element_type=F32,
            )
            if first[0]:
                acc[p] = term
            else:
                acc[p] += term
        first[0] = False

    conv(0)
    for step in range(1, 4):
        for s in range(2):
            for way in range(2):
                ring_send(step - 1, s, way).wait_recv()
                slot = -step % 8 if way == 0 else step
                if step < 3 or s == way:
                    go(ring_send(step, s, way))
                go(hand_over(slot, s))
        if step == 3:
            x_own.wait()
            for c in x_sends:
                c.wait_recv()
            x_hand = remote(xt.at[half], xt.at[half], xs_s, xs_r, sib)
            go(x_hand)
        conv(step)
        conv(-step)
    for way in range(2):
        ring_send(3, way, way).wait_recv()
        go(hand_over(4, way))
    conv(4)

    for p in range(4):
        for e in range(2):
            for k in range(3):
                corr[(2 * p + e) * B:(2 * p + e + 1) * B, k * B:(k + 1) * B] = acc[
                    p, k * B:(k + 1) * B, e * B:(e + 1) * B
                ].astype(BF16)

    half_o = pl.ds((1 - core) * 4, 4)
    remote(xt.at[half_o], xt.at[half_o], xs_s, xs_r, sib).wait_recv()
    for zz in range(8):
        part = jnp.dot(xt[zz], corr[...], preferred_element_type=F32).astype(BF16)
        for k in range(3):
            pgb[zz, k] = part[:, k * B:(k + 1) * B]

    def at(o):
        return lax.rem(z + o + 8, 8)

    def sum_send(step, k, way):
        src = pgb.at[at(4 if way == 0 else -3), k] if step == 0 else pgs.at[way, step - 1, k]
        return remote(
            src, pgr.at[way, step, k], pr_s.at[way, step, k], pr_r.at[way, step, k],
            up if way == 0 else down,
        )

    def sum_step(step):
        for k in range(3):
            for way in range(2):
                if way == 1 and step == 3:
                    continue
                sum_send(step - 1, k, way).wait_recv()
                o = 4 - step if way == 0 else step - 3
                pgs[way, step - 1, k] = (
                    pgr[way, step - 1, k].astype(F32) + pgb[at(o), k].astype(F32)
                ).astype(BF16)
                go(sum_send(step, k, way))

    for k in range(3):
        for way in range(2):
            go(sum_send(0, k, way))

    for p in p_copies:
        p.wait()

    def tile(x_to, of_core):
        cols = pl.ds(pl.multiple_of(x_to * 512 + of_core * 256, 256), 256)
        return lax.dot_general(
            corr[...], pn[cols, :], (((1,), (1,)), ((), ())), preferred_element_type=F32
        )

    swaps = []
    for x_to in range(2):
        igs[x_to] = tile(x_to, 1 - core).astype(BF16).reshape(8, B, 256)
        swaps.append(remote(igs.at[x_to], igr.at[x_to], is_s.at[x_to], is_r.at[x_to], sib))
        go(swaps[-1])
    sum_step(1)
    for x_to in range(2):
        igo[x_to] = tile(x_to, core).reshape(8, B, 256)
    sum_step(2)
    for x_to in range(2):
        swaps[x_to].wait_recv()
        igc[x_to] = (igo[x_to] + igr[x_to].astype(F32)).astype(BF16)
    ig_sends = []
    for r in range(1, 16):
        dx, dq = r // 8, r % 8
        ig_sends.append(
            remote(
                igc.at[lax.rem(xh + dx, 2), lax.rem(q + dq, 8)], igd.at[r],
                id_s.at[r], id_r.at[r], plane(dx, dq),
            )
        )
        go(ig_sends[-1])
    sum_step(3)

    scale = 8192.0 ** -0.5
    for k in range(3):
        sum_send(2, k, 1).wait_recv()
        sum_send(3, k, 0).wait_recv()
        total = (
            pgr[0, 3, k].astype(F32) + pgr[1, 2, k].astype(F32) + pgb[z, k].astype(F32)
        ) * scale
        pga[:, k] = total.astype(BF16).reshape(8, 16, B)
    pg_sends = []
    for r in range(1, 8):
        pg_sends.append(
            remote(
                pga.at[lax.rem(q + r, 8)], pgo.at[q], pa_s.at[r], pa_r.at[r], plane(0, r)
            )
        )
        go(pg_sends[-1])
    pgo[q] = pga[q]

    for c in ig_sends:
        c.wait_recv()
    total = igc[xh, q].astype(F32)
    for r in range(1, 16):
        total = total + igd[r].astype(F32)
    ig_ref[...] = total.astype(BF16)

    for c in pg_sends:
        c.wait_recv()
    for s in range(8):
        pg_ref[:, :, s * B:(s + 1) * B] = pgo[s]
    for c in sent:
        c.wait_send()


def per_device(inputs, cotangent, filters, projections):
    vmem = pl.BlockSpec(memory_space=pltpu.VMEM)
    dma = pltpu.SemaphoreType.DMA
    return pl.pallas_call(
        kernel,
        out_shape=(
            jax.ShapeDtypeStruct((B, 256), BF16),
            jax.ShapeDtypeStruct((3, 16, 1024), BF16),
        ),
        in_specs=[vmem, vmem, vmem, pl.BlockSpec(memory_space=pl.ANY)],
        out_specs=(vmem, vmem),
        scratch_shapes=[
            pltpu.VMEM((8, 8192), F32),
            pltpu.VMEM((8, 384, 1024), BF16),
            pltpu.VMEM((8, 2, 8, 64, B), BF16),
            pltpu.VMEM((1, 1152, 256), BF16),
            pltpu.VMEM((4, 384, 256), F32),
            pltpu.VMEM((1024, 384), BF16),
            pltpu.VMEM((8, B, B), BF16),
            pltpu.VMEM((8, B, 1024), BF16),
            pltpu.VMEM((1024, 384), BF16),
            pltpu.VMEM((8, 3, B, B), BF16),
            pltpu.VMEM((2, 4, 3, B, B), BF16),
            pltpu.VMEM((2, 3, 3, B, B), BF16),
            pltpu.VMEM((8, 3, 16, B), BF16),
            pltpu.VMEM((8, 3, 16, B), BF16),
            pltpu.VMEM((2, 8, B, 256), BF16),
            pltpu.VMEM((2, 8, B, 256), BF16),
            pltpu.VMEM((2, 8, B, 256), F32),
            pltpu.VMEM((2, 8, B, 256), BF16),
            pltpu.VMEM((16, B, 256), BF16),
            dma((8,)), dma((8,)),
            dma((2, 4, 2)), dma((2, 4, 2)),
            dma((8, 2)), dma((8, 2)),
            dma((8,)), dma((8,)),
            dma, dma,
            dma((4,)),
            dma((2, 4, 3)), dma((2, 4, 3)),
            dma((8,)), dma((8,)),
            dma((2,)), dma((2,)),
            dma((16,)), dma((16,)),
        ],
        compiler_params=pltpu.CompilerParams(
            collective_id=0, has_side_effects=True, vmem_limit_bytes=48 * 1024 * 1024
        ),
        cost_estimate=pl.CostEstimate(
            flops=6_000_000_000, bytes_accessed=2_000_000, transcendentals=0
        ),
    )(inputs, cotangent, filters, projections)


def solution(mesh):
    placed = (P("seq", None), P("seq", None), P(), P("filt", None, None))
    return jax.shard_map(
        per_device,
        mesh=mesh,
        in_specs=placed,
        out_specs=(P("seq", "filt"), P("filt", "seq", None)),
        check_vma=False,
    )
```

```python
import functools

import jax
import jax.numpy as jnp
from jax import lax
from jax.experimental import pallas as pl
from jax.experimental.pallas import tpu as pltpu
from jax.sharding import PartitionSpec as P

MESH = pl.DeviceIdType.MESH
F32 = jnp.float32
BF16 = jnp.bfloat16
B = 128
ORDER = (0, 1, -1, 2, -2, 3, -3, 4)


def kernel(
    x_ref, g_ref, f_ref, p_ref, ig_ref, pg_ref,
    taps, fv, gv, xv, hank, gl, g2, acc, corr, xs, xt, pn, pgb, pgr, pgs, pga, pgo,
    igs, igr, igo, igc, igd,
    ga_s, ga_r, gr_s, gr_r, gs_s, gs_r, xa_s, xa_r, xs_s, xs_r, loc,
    pr_s, pr_r, pa_s, pa_r, is_s, is_r, id_s, id_r,
):
    seq = lax.axis_index("seq")
    filt = lax.axis_index("filt")
    q, z = lax.div(seq, 8), lax.rem(seq, 8)
    xh, core = lax.div(filt, 2), lax.rem(filt, 2)
    sib = (seq, xh * 2 + 1 - core)
    up = (q * 8 + lax.rem(z + 1, 8), filt)
    down = (q * 8 + lax.rem(z + 7, 8), filt)

    def plane(dx, dq):
        return (lax.rem(q + dq, 8) * 8 + z, lax.rem(xh + dx, 2) * 2 + core)

    def remote(src, dst, send, recv, to):
        return pltpu.make_async_remote_copy(
            src_ref=src, dst_ref=dst, send_sem=send, recv_sem=recv,
            device_id=to, device_id_type=MESH,
        )

    sent = []

    def go(copy):
        copy.start()
        sent.append(copy)

    barrier = pltpu.get_barrier_semaphore()
    partners = [sib, up, down] + [plane(r // 8, r % 8) for r in range(1, 16)]
    for to in partners:
        pl.semaphore_signal(barrier, inc=1, device_id=to, device_id_type=MESH)

    rows = pl.ds(pl.multiple_of(core * 64, 64), 64)
    lanes = pl.ds(pl.multiple_of(q * B, B), B)
    f_in = pltpu.make_async_copy(f_ref, fv, loc.at[4])
    g_in = pltpu.make_async_copy(g_ref.at[rows], gv, loc.at[5])
    g_own = pltpu.make_async_copy(g_ref.at[rows, lanes], gl.at[0, core, q], loc.at[6])
    x_in = pltpu.make_async_copy(x_ref, xv, loc.at[7])
    p_copies = [
        pltpu.make_async_copy(p_ref.at[k, :, lanes], pn.at[:, pl.ds(k * B, B)], loc.at[k])
        for k in range(3)
    ]
    for c in [f_in, g_in, g_own, x_in] + p_copies:
        c.start()
    f_in.wait()
    pick = jnp.where(
        lax.broadcasted_iota(jnp.int32, (8, 12), 1)
        == lax.broadcasted_iota(jnp.int32, (8, 12), 0) + 3 * filt,
        1.0, 0.0,
    ).astype(BF16)
    taps[:, 0:B] = jnp.zeros((8, B), F32)
    taps[:, B:] = jnp.dot(pick, fv[...], preferred_element_type=F32)
    g2[0, 1024:1152, 0:B] = jnp.zeros((B, B), BF16)
    g2[0, 896:1152, B:2 * B] = jnp.zeros((2 * B, B), BF16)

    def build(j, carry):
        for i in range(8):
            upper = lax.broadcasted_iota(jnp.int32, (16, B), 1) >= (
                lax.broadcasted_iota(jnp.int32, (16, B), 0) + 16 * i
            )
            for k in range(3):
                before = None
                for d in range(-1, 8):
                    row = taps[k:k + 1, pl.ds(pl.multiple_of((8 * j + d + 1) * B, B), B)]
                    turned = pltpu.roll(
                        jnp.broadcast_to(row, (16, B)), 16 * i, 1, stride=1, stride_axis=0
                    )
                    if d >= 0:
                        hank[d, k * B + 16 * i:k * B + 16 * i + 16,
                             pl.ds(pl.multiple_of(j * B, B), B)] = jnp.where(
                                 upper, turned, before
                             ).astype(BF16)
                    before = turned
        return carry

    lax.fori_loop(0, 4, build, 0)
    g_in.wait()
    g_own.wait()

    pl.semaphore_wait(barrier, len(partners))

    a2a = []
    for r in range(1, 8):
        col = pl.ds(pl.multiple_of(lax.rem(q + r, 8) * B, B), B)
        a2a.append(
            remote(gv.at[:, col], gl.at[0, core, q], ga_s.at[r], ga_r.at[r], plane(0, r))
        )
        go(a2a[-1])
    lax.fori_loop(4, 8, build, 0)

    x_in.wait()
    for t in range(8):
        flip = xv[:, t * B:(t + 1) * B].T
        for zz in range(8):
            xs[zz, t * 16:(t + 1) * 16, :] = flip[zz * 16:(zz + 1) * 16]
    half = pl.ds(core * 4, 4)
    x_own = pltpu.make_async_copy(xs.at[half], xt.at[half, :, lanes], loc.at[3])
    x_own.start()

    def sub(slot, s):
        return gl.at[slot, core, pl.ds(s * 2, 2)]

    def ring_send(step, s, way):
        here = -step % 8 if way == 0 else step
        there = (-step - 1) % 8 if way == 0 else step + 1
        return remote(
            sub(here, s), sub(there, s),
            gr_s.at[way, step, s], gr_r.at[way, step, s], up if way == 0 else down,
        )

    def hand_over(slot):
        mine = gl.at[slot, core]
        return remote(mine, mine, gs_s.at[slot], gs_r.at[slot], sib)

    def handed(slot):
        other = gl.at[slot, 1 - core]
        return remote(other, other, gs_s.at[slot], gs_r.at[slot], sib)

    for c in a2a:
        c.wait_recv()
    for s in range(4):
        for way in range(2):
            go(ring_send(0, s, way))
    go(hand_over(0))

    x_sends = []
    for r in range(1, 8):
        x_sends.append(
            remote(xs.at[half], xt.at[half, :, lanes], xa_s.at[r], xa_r.at[r], plane(0, r))
        )
        go(x_sends[-1])

    def conv(o):
        slot = o % 8
        handed(slot).wait_recv()
        buf = g2.at[0]
        for m in range(8):
            for h in range(2):
                piece = gl[slot, h, m]
                buf[m * B + h * 64:m * B + h * 64 + 64, 0:B] = piece
                if m > 0:
                    buf[(m - 1) * B + h * 64:(m - 1) * B + h * 64 + 64, B:2 * B] = piece
        wrap = jnp.where(lax.rem(z + o + 8, 8) < z, 1, 0)
        for p in range(4):
            depth = B * (8 - 2 * p)
            start = pl.multiple_of(wrap * B + 2 * p * B, B)
            term = jnp.dot(
                hank[slot, :, 0:depth], buf[pl.ds(start, depth), :],
                preferred_element_type=F32,
            )
            if o == 0:
                acc[p] = term
            elif o != 4:
                acc[p] += term
            else:
                done = (acc[p] + term).astype(BF16)
                for e in range(2):
                    for k in range(3):
                        corr[(2 * p + e) * B:(2 * p + e + 1) * B, k * B:(k + 1) * B] = done[
                            k * B:(k + 1) * B, e * B:(e + 1) * B
                        ]

    conv(0)
    for step in range(1, 4):
        for s in range(4):
            for way in range(2):
                ring_send(step - 1, s, way).wait_recv()
                if step < 3 or s // 2 == way:
                    go(ring_send(step, s, way))
        go(hand_over(-step % 8))
        go(hand_over(step))
        if step > 1:
            conv(step - 1)
            conv(1 - step)
        if step == 3:
            x_own.wait()
            for c in x_sends:
                c.wait_recv()
            x_hand = remote(xt.at[half], xt.at[half], xs_s, xs_r, sib)
            go(x_hand)
    for s in range(4):
        ring_send(3, s, s // 2).wait_recv()
    go(hand_over(4))
    conv(3)
    conv(-3)
    conv(4)

    half_o = pl.ds((1 - core) * 4, 4)
    remote(xt.at[half_o], xt.at[half_o], xs_s, xs_r, sib).wait_recv()
    def at(o):
        return lax.rem(z + o + 8, 8)

    def sum_send(step, k, way):
        src = pgb.at[at(4 if way == 0 else -3), k] if step == 0 else pgs.at[way, step - 1, k]
        return remote(
            src, pgr.at[way, step, k], pr_s.at[way, step, k], pr_r.at[way, step, k],
            up if way == 0 else down,
        )

    def sum_step(step):
        for k in range(3):
            for way in range(2):
                if way == 1 and step == 3:
                    continue
                sum_send(step - 1, k, way).wait_recv()
                o = 4 - step if way == 0 else step - 3
                pgs[way, step - 1, k] = (
                    pgr[way, step - 1, k].astype(F32) + pgb[at(o), k].astype(F32)
                ).astype(BF16)
                go(sum_send(step, k, way))

    for o in (4, -3, 3, -2, 2, -1, 1, 0):
        part = jnp.dot(xt[at(o)], corr[...], preferred_element_type=F32).astype(BF16)
        for k in range(3):
            pgb[at(o), k] = part[:, k * B:(k + 1) * B]
        if o == -3:
            for k in range(3):
                for way in range(2):
                    go(sum_send(0, k, way))

    for p in p_copies:
        p.wait()

    def tile(x_to, of_core):
        cols = pl.ds(pl.multiple_of(x_to * 512 + of_core * 256, 256), 256)
        return lax.dot_general(
            corr[...], pn[cols, :], (((1,), (1,)), ((), ())), preferred_element_type=F32
        )

    swaps = []
    for x_to in range(2):
        igs[x_to] = tile(x_to, 1 - core).astype(BF16).reshape(8, B, 256)
        swaps.append(remote(igs.at[x_to], igr.at[x_to], is_s.at[x_to], is_r.at[x_to], sib))
        go(swaps[-1])
    sum_step(1)
    for x_to in range(2):
        igo[x_to] = tile(x_to, core).reshape(8, B, 256)
    sum_step(2)
    for x_to in range(2):
        swaps[x_to].wait_recv()
        igc[x_to] = (igo[x_to] + igr[x_to].astype(F32)).astype(BF16)
    ig_sends = []
    for r in range(1, 16):
        dx, dq = r // 8, r % 8
        ig_sends.append(
            remote(
                igc.at[lax.rem(xh + dx, 2), lax.rem(q + dq, 8)], igd.at[r],
                id_s.at[r], id_r.at[r], plane(dx, dq),
            )
        )
        go(ig_sends[-1])
    sum_step(3)

    scale = 8192.0 ** -0.5
    for k in range(3):
        sum_send(2, k, 1).wait_recv()
        sum_send(3, k, 0).wait_recv()
        total = (
            pgr[0, 3, k].astype(F32) + pgr[1, 2, k].astype(F32) + pgb[z, k].astype(F32)
        ) * scale
        pga[:, k] = total.astype(BF16).reshape(8, 16, B)
    pg_sends = []
    for r in range(1, 8):
        pg_sends.append(
            remote(
                pga.at[lax.rem(q + r, 8)], pgo.at[q], pa_s.at[r], pa_r.at[r], plane(0, r)
            )
        )
        go(pg_sends[-1])
    pgo[q] = pga[q]

    for c in ig_sends:
        c.wait_recv()
    total = igc[xh, q].astype(F32)
    for r in range(1, 16):
        total = total + igd[r].astype(F32)
    ig_ref[...] = total.astype(BF16)

    for c in pg_sends:
        c.wait_recv()
    for s in range(8):
        pg_ref[:, :, s * B:(s + 1) * B] = pgo[s]
    for c in sent:
        c.wait_send()


def per_device(inputs, cotangent, filters, projections):
    vmem = pl.BlockSpec(memory_space=pltpu.VMEM)
    dma = pltpu.SemaphoreType.DMA
    return pl.pallas_call(
        kernel,
        out_shape=(
            jax.ShapeDtypeStruct((B, 256), BF16),
            jax.ShapeDtypeStruct((3, 16, 1024), BF16),
        ),
        in_specs=[pl.BlockSpec(memory_space=pl.ANY)] * 4,
        out_specs=(vmem, vmem),
        scratch_shapes=[
            pltpu.VMEM((8, 8192 + B), F32),
            pltpu.VMEM((12, 8192), BF16),
            pltpu.VMEM((64, 1024), BF16),
            pltpu.VMEM((B, 1024), BF16),
            pltpu.VMEM((8, 384, 1024), BF16),
            pltpu.VMEM((8, 2, 8, 64, B), BF16),
            pltpu.VMEM((1, 1152, 256), BF16),
            pltpu.VMEM((4, 384, 256), F32),
            pltpu.VMEM((1024, 384), BF16),
            pltpu.VMEM((8, B, B), BF16),
            pltpu.VMEM((8, B, 1024), BF16),
            pltpu.VMEM((1024, 384), BF16),
            pltpu.VMEM((8, 3, B, B), BF16),
            pltpu.VMEM((2, 4, 3, B, B), BF16),
            pltpu.VMEM((2, 3, 3, B, B), BF16),
            pltpu.VMEM((8, 3, 16, B), BF16),
            pltpu.VMEM((8, 3, 16, B), BF16),
            pltpu.VMEM((2, 8, B, 256), BF16),
            pltpu.VMEM((2, 8, B, 256), BF16),
            pltpu.VMEM((2, 8, B, 256), F32),
            pltpu.VMEM((2, 8, B, 256), BF16),
            pltpu.VMEM((16, B, 256), BF16),
            dma((8,)), dma((8,)),
            dma((2, 4, 4)), dma((2, 4, 4)),
            dma((8,)), dma((8,)),
            dma((8,)), dma((8,)),
            dma, dma,
            dma((8,)),
            dma((2, 4, 3)), dma((2, 4, 3)),
            dma((8,)), dma((8,)),
            dma((2,)), dma((2,)),
            dma((16,)), dma((16,)),
        ],
        compiler_params=pltpu.CompilerParams(
            collective_id=0, has_side_effects=True, vmem_limit_bytes=58 * 1024 * 1024
        ),
        cost_estimate=pl.CostEstimate(
            flops=6_000_000_000, bytes_accessed=2_000_000, transcendentals=0
        ),
    )(inputs, cotangent, filters, projections)


def solution(mesh):
    placed = (P("seq", None), P("seq", None), P(), P("filt", None, None))
    return jax.shard_map(
        per_device,
        mesh=mesh,
        in_specs=placed,
        out_specs=(P("seq", "filt"), P("filt", "seq", None)),
        check_vma=False,
    )
```

```python
import functools

import jax
import jax.numpy as jnp
from jax import lax
from jax.experimental import pallas as pl
from jax.experimental.pallas import tpu as pltpu
from jax.sharding import PartitionSpec as P

MESH = pl.DeviceIdType.MESH
F32 = jnp.float32
BF16 = jnp.bfloat16
B = 128
ORDER = (0, 1, -1, 2, -2, 3, -3, 4)


def kernel(
    x_ref, g_ref, f_ref, p_ref, ig_ref, pg_ref,
    taps, fv, xv, hank, gl, g2, acc, corr, xs, xt, pn, pgb, pgr, pgs, pga, pgo, pgp,
    igs, igr, igo, igc, igd,
    ga_s, ga_r, gr_s, gr_r, gs_s, gs_r, ge_s, ge_r, xa_s, xa_r, xs_s, xs_r, loc,
    pr_s, pr_r, pa_s, pa_r, is_s, is_r, id_s, id_r,
):
    seq = lax.axis_index("seq")
    filt = lax.axis_index("filt")
    q, z = lax.div(seq, 8), lax.rem(seq, 8)
    xh, core = lax.div(filt, 2), lax.rem(filt, 2)
    sib = (seq, xh * 2 + 1 - core)
    up = (q * 8 + lax.rem(z + 1, 8), filt)
    down = (q * 8 + lax.rem(z + 7, 8), filt)

    def plane(dx, dq):
        return (lax.rem(q + dq, 8) * 8 + z, lax.rem(xh + dx, 2) * 2 + core)

    def remote(src, dst, send, recv, to):
        return pltpu.make_async_remote_copy(
            src_ref=src, dst_ref=dst, send_sem=send, recv_sem=recv,
            device_id=to, device_id_type=MESH,
        )

    sent = []

    def go(copy):
        copy.start()
        sent.append(copy)

    def near(dz, dq):
        return (lax.rem(q + dq, 8) * 8 + lax.rem(z + dz + 8, 8), filt)

    barrier = pltpu.get_barrier_semaphore()
    partners = (
        [sib]
        + [plane(r // 8, r % 8) for r in range(1, 16)]
        + [near(dz, r) for dz in (1, -1) for r in range(8)]
    )
    for to in partners:
        pl.semaphore_signal(barrier, inc=1, device_id=to, device_id_type=MESH)

    rows = pl.ds(pl.multiple_of(core * 64, 64), 64)
    lanes = pl.ds(pl.multiple_of(q * B, B), B)
    f_in = pltpu.make_async_copy(f_ref, fv, loc.at[4])
    g_own = pltpu.make_async_copy(g_ref.at[rows, lanes], gl.at[0, core, q], loc.at[6])
    x_in = pltpu.make_async_copy(x_ref, xv, loc.at[7])
    p_copies = [
        pltpu.make_async_copy(p_ref.at[k, :, lanes], pn.at[:, pl.ds(k * B, B)], loc.at[k])
        for k in range(3)
    ]
    for c in [f_in, g_own, x_in] + p_copies:
        c.start()
    f_in.wait()
    pick = jnp.where(
        lax.broadcasted_iota(jnp.int32, (8, 12), 1)
        == lax.broadcasted_iota(jnp.int32, (8, 12), 0) + 3 * filt,
        1.0, 0.0,
    ).astype(BF16)
    taps[:, 0:B] = jnp.zeros((8, B), F32)
    taps[:, B:] = jnp.dot(pick, fv[...], preferred_element_type=F32)
    g2[0, 1024:1152, 0:B] = jnp.zeros((B, B), BF16)
    g2[0, 896:1152, B:2 * B] = jnp.zeros((2 * B, B), BF16)

    def build(j, carry):
        for i in range(8):
            upper = lax.broadcasted_iota(jnp.int32, (16, B), 1) >= (
                lax.broadcasted_iota(jnp.int32, (16, B), 0) + 16 * i
            )
            for k in range(3):
                before = None
                for d in range(-1, 8):
                    row = taps[k:k + 1, pl.ds(pl.multiple_of((8 * j + d + 1) * B, B), B)]
                    turned = pltpu.roll(
                        jnp.broadcast_to(row, (16, B)), 16 * i, 1, stride=1, stride_axis=0
                    )
                    if d >= 0:
                        hank[d, k * B + 16 * i:k * B + 16 * i + 16,
                             pl.ds(pl.multiple_of(j * B, B), B)] = jnp.where(
                                 upper, turned, before
                             ).astype(BF16)
                    before = turned
        return carry

    lax.fori_loop(0, 4, build, 0)
    g_own.wait()

    pl.semaphore_wait(barrier, len(partners))

    pieces = []
    for r in range(8):
        col = pl.ds(pl.multiple_of(lax.rem(q + r, 8) * B, B), B)
        for d, dz in ((1, 1), (2, -1), (0, 0)):
            if r == 0 and dz == 0:
                continue
            c = remote(
                g_ref.at[rows, col], gl.at[-dz % 8, core, q], ga_s.at[d, r],
                ga_r.at[d, r if dz == 0 else q], near(dz, r),
            )
            go(c)
            if dz == 0:
                pieces.append(c)
    lax.fori_loop(4, 8, build, 0)

    x_in.wait()
    for t in range(8):
        flip = xv[:, t * B:(t + 1) * B].T
        for zz in range(8):
            xs[zz, t * 16:(t + 1) * 16, :] = flip[zz * 16:(zz + 1) * 16]
    half = pl.ds(core * 4, 4)
    x_own = pltpu.make_async_copy(xs.at[half], xt.at[half, :, lanes], loc.at[3])
    x_own.start()

    def sub(slot, s):
        return gl.at[slot, core, pl.ds(s * 2, 2)]

    def ring_send(step, s, way):
        here = -step % 8 if way == 0 else step
        there = (-step - 1) % 8 if way == 0 else step + 1
        return remote(
            sub(here, s), sub(there, s),
            gr_s.at[way, step, s], gr_r.at[way, step, s], up if way == 0 else down,
        )

    def hand_over(slot):
        mine = gl.at[slot, core]
        return remote(mine, mine, gs_s.at[slot], gs_r.at[slot], sib)

    def handed(slot):
        other = gl.at[slot, 1 - core]
        return remote(other, other, gs_s.at[slot], gs_r.at[slot], sib)

    def landed(d, m):
        here = gl.at[-1 % 8 if d == 1 else 1, core, m]
        return remote(here, here, ga_s.at[d, 0], ga_r.at[d, m], up)

    for c in pieces:
        c.wait_recv()
    go(hand_over(0))
    for s in range(4):
        for way in range(2):
            landed(way + 1, 2 * s).wait_recv()
            landed(way + 1, 2 * s + 1).wait_recv()
            go(ring_send(1, s, way))
    go(hand_over(-1 % 8))
    go(hand_over(1))

    x_sends = []
    for r in range(1, 8):
        x_sends.append(
            remote(xs.at[half], xt.at[half, :, lanes], xa_s.at[r], xa_r.at[r], plane(0, r))
        )
        go(x_sends[-1])

    def conv(o):
        slot = o % 8
        if o == 4:
            for s in range(4):
                other = gl.at[4, 1 - core, pl.ds(s * 2, 2)]
                remote(other, other, ge_s.at[s], ge_r.at[s], sib).wait_recv()
        else:
            handed(slot).wait_recv()
        buf = g2.at[0]
        for m in range(8):
            for h in range(2):
                piece = gl[slot, h, m]
                buf[m * B + h * 64:m * B + h * 64 + 64, 0:B] = piece
                if m > 0:
                    buf[(m - 1) * B + h * 64:(m - 1) * B + h * 64 + 64, B:2 * B] = piece
        wrap = jnp.where(lax.rem(z + o + 8, 8) < z, 1, 0)
        for p in range(4):
            depth = B * (8 - 2 * p)
            start = pl.multiple_of(wrap * B + 2 * p * B, B)
            term = jnp.dot(
                hank[slot, :, 0:depth], buf[pl.ds(start, depth), :],
                preferred_element_type=F32,
            )
            if o == 0:
                acc[p] = term
            elif o != 4:
                acc[p] += term
            else:
                done = (acc[p] + term).astype(BF16)
                for e in range(2):
                    for k in range(3):
                        corr[(2 * p + e) * B:(2 * p + e + 1) * B, k * B:(k + 1) * B] = done[
                            k * B:(k + 1) * B, e * B:(e + 1) * B
                        ]

    conv(0)
    for step in range(2, 4):
        for s in range(4):
            for way in range(2):
                ring_send(step - 1, s, way).wait_recv()
                if step < 3 or s // 2 == way:
                    go(ring_send(step, s, way))
        go(hand_over(-step % 8))
        go(hand_over(step))
        conv(step - 1)
        conv(1 - step)
        if step == 3:
            x_own.wait()
            for c in x_sends:
                c.wait_recv()
            x_hand = remote(xt.at[half], xt.at[half], xs_s, xs_r, sib)
            go(x_hand)
    conv(3)
    for s in range(4):
        ring_send(3, s, s // 2).wait_recv()
        mine = sub(4, s)
        go(remote(mine, mine, ge_s.at[s], ge_r.at[s], sib))
    conv(-3)
    conv(4)

    for p in p_copies:
        p.wait()

    def tile(x_to, of_core, upper_half):
        cols = pl.ds(pl.multiple_of(x_to * 512 + of_core * 256, 256), 256)
        return lax.dot_general(
            corr[upper_half * 512:upper_half * 512 + 512], pn[cols, :],
            (((1,), (1,)), ((), ())), preferred_element_type=F32,
        ).reshape(4, B, 256)

    quarters = [(x_to, u) for u in range(2) for x_to in range(2)]
    swaps = []
    for n, (x_to, u) in enumerate(quarters):
        part = pl.ds(u * 4, 4)
        igs[x_to, part] = tile(x_to, 1 - core, u).astype(BF16)
        swaps.append(
            remote(igs.at[x_to, part], igr.at[x_to, part], is_s.at[n], is_r.at[n], sib)
        )
        go(swaps[-1])

    half_o = pl.ds((1 - core) * 4, 4)
    remote(xt.at[half_o], xt.at[half_o], xs_s, xs_r, sib).wait_recv()

    def at(o):
        return lax.rem(z + o + 8, 8)

    def products(*offsets):
        for o in offsets:
            part = jnp.dot(xt[at(o)], corr[...], preferred_element_type=F32).astype(BF16)
            for k in range(3):
                if o == 0:
                    pgo[:, k] = part[:, k * B:(k + 1) * B].reshape(8, 16, B)
                else:
                    pgb[at(o), k] = part[:, k * B:(k + 1) * B]

    def sum_send(step, k, way):
        src = pgb.at[at(4 if way == 0 else -3), k] if step == 0 else pgs.at[way, step - 1, k]
        return remote(
            src, pgr.at[way, step, k], pr_s.at[way, step, k], pr_r.at[way, step, k],
            up if way == 0 else down,
        )

    def sum_step(step, way):
        last = step == (3 if way == 0 else 2)
        o = 4 - step if way == 0 else step - 3
        for k in range(3):
            sum_send(step - 1, k, way).wait_recv()
            total = (
                pgr[way, step - 1, k].astype(F32) + pgb[at(o), k].astype(F32)
            ).astype(BF16)
            if last:
                pga[way, :, k] = total.reshape(8, 16, B)
            else:
                pgs[way, step - 1, k] = total
                go(sum_send(step, k, way))
        if last:
            for r in range(8):
                go(remote(
                    pga.at[way, lax.rem(q + r, 8)], pgp.at[way + 1, q],
                    pa_s.at[way + 1, r], pa_r.at[way + 1, q], near(1 if way == 0 else -1, r),
                ))

    products(4, -3)
    for k in range(3):
        for way in range(2):
            go(sum_send(0, k, way))
    for n, (x_to, u) in enumerate(quarters):
        igo[x_to, u * 4:u * 4 + 4] = tile(x_to, core, u)
    products(3, -2)

    ig_sends = []
    for n, (x_to, u) in enumerate(quarters):
        part = pl.ds(u * 4, 4)
        swaps[n].wait_recv()
        igc[x_to, part] = (igo[x_to, part] + igr[x_to, part].astype(F32)).astype(BF16)
    for r in range(1, 16):
        dx, dq = r // 8, r % 8
        ig_sends.append(
            remote(
                igc.at[lax.rem(xh + dx, 2), lax.rem(q + dq, 8)], igd.at[r],
                id_s.at[r], id_r.at[r], plane(dx, dq),
            )
        )
        go(ig_sends[-1])

    sum_step(1, 0)
    sum_step(1, 1)
    products(0, 2, -1, 1)
    pg_sends = []
    for r in range(1, 8):
        pg_sends.append(
            remote(
                pgo.at[lax.rem(q + r, 8)], pgp.at[0, q], pa_s.at[0, r], pa_r.at[0, r],
                plane(0, r),
            )
        )
        go(pg_sends[-1])
    pgp[0, q] = pgo[q]
    sum_step(2, 0)
    sum_step(2, 1)
    sum_step(3, 0)

    total = igc[xh, q].astype(F32)
    for r in range(1, 16):
        ig_sends[r - 1].wait_recv()
        total = total + igd[r].astype(F32)
    ig_ref[...] = total.astype(BF16)

    for c in pg_sends:
        c.wait_recv()
    for s in range(8):
        for d in (1, 2):
            here = pgp.at[d, s]
            remote(here, here, pa_s.at[d, 0], pa_r.at[d, s], up).wait_recv()
        total = (
            pgp[0, s].astype(F32) + pgp[1, s].astype(F32) + pgp[2, s].astype(F32)
        ) * (8192.0 ** -0.5)
        pg_ref[:, :, s * B:(s + 1) * B] = total.astype(BF16)
    for c in sent:
        c.wait_send()


def per_device(inputs, cotangent, filters, projections):
    vmem = pl.BlockSpec(memory_space=pltpu.VMEM)
    dma = pltpu.SemaphoreType.DMA
    return pl.pallas_call(
        kernel,
        out_shape=(
            jax.ShapeDtypeStruct((B, 256), BF16),
            jax.ShapeDtypeStruct((3, 16, 1024), BF16),
        ),
        in_specs=[pl.BlockSpec(memory_space=pltpu.HBM)] * 4,
        out_specs=(vmem, vmem),
        scratch_shapes=[
            pltpu.VMEM((8, 8192 + B), F32),
            pltpu.VMEM((12, 8192), BF16),
            pltpu.VMEM((B, 1024), BF16),
            pltpu.VMEM((8, 384, 1024), BF16),
            pltpu.VMEM((8, 2, 8, 64, B), BF16),
            pltpu.VMEM((1, 1152, 256), BF16),
            pltpu.VMEM((4, 384, 256), F32),
            pltpu.VMEM((1024, 384), BF16),
            pltpu.VMEM((8, B, B), BF16),
            pltpu.VMEM((8, B, 1024), BF16),
            pltpu.VMEM((1024, 384), BF16),
            pltpu.VMEM((8, 3, B, B), BF16),
            pltpu.VMEM((2, 4, 3, B, B), BF16),
            pltpu.VMEM((2, 2, 3, B, B), BF16),
            pltpu.VMEM((2, 8, 3, 16, B), BF16),
            pltpu.VMEM((8, 3, 16, B), BF16),
            pltpu.VMEM((3, 8, 3, 16, B), BF16),
            pltpu.VMEM((2, 8, B, 256), BF16),
            pltpu.VMEM((2, 8, B, 256), BF16),
            pltpu.VMEM((2, 8, B, 256), F32),
            pltpu.VMEM((2, 8, B, 256), BF16),
            pltpu.VMEM((16, B, 256), BF16),
            dma((3, 8)), dma((3, 8)),
            dma((2, 4, 4)), dma((2, 4, 4)),
            dma((8,)), dma((8,)),
            dma((4,)), dma((4,)),
            dma((8,)), dma((8,)),
            dma, dma,
            dma((8,)),
            dma((2, 4, 3)), dma((2, 4, 3)),
            dma((3, 8)), dma((3, 8)),
            dma((4,)), dma((4,)),
            dma((16,)), dma((16,)),
        ],
        compiler_params=pltpu.CompilerParams(
            collective_id=0, has_side_effects=True, vmem_limit_bytes=48 * 1024 * 1024
        ),
        cost_estimate=pl.CostEstimate(
            flops=6_000_000_000, bytes_accessed=2_000_000, transcendentals=0
        ),
    )(inputs, cotangent, filters, projections)


def solution(mesh):
    placed = (P("seq", None), P("seq", None), P(), P("filt", None, None))
    return jax.shard_map(
        per_device,
        mesh=mesh,
        in_specs=placed,
        out_specs=(P("seq", "filt"), P("filt", "seq", None)),
        check_vma=False,
    )
```

```python
import functools

import jax
import jax.numpy as jnp
from jax import lax
from jax.experimental import pallas as pl
from jax.experimental.pallas import tpu as pltpu
from jax.sharding import PartitionSpec as P

MESH = pl.DeviceIdType.MESH
F32 = jnp.float32
BF16 = jnp.bfloat16
B = 128
ORDER = (0, 1, -1, 2, -2, 3, -3, 4)


def kernel(
    x_ref, g_ref, f_ref, p_ref, ig_ref, pg_ref,
    taps, fv, gv, xv, hank, gl, g2, acc, corr, xs, xt, pn, pgb, pgr, pgs, pga, pgo, pgp,
    igs, igr, igo, igc, igd,
    ga_s, ga_r, gr_s, gr_r, gs_s, gs_r, ge_s, ge_r, xa_s, xa_r, xs_s, xs_r, loc,
    pr_s, pr_r, pa_s, pa_r, is_s, is_r, id_s, id_r,
):
    seq = lax.axis_index("seq")
    filt = lax.axis_index("filt")
    q, z = lax.div(seq, 8), lax.rem(seq, 8)
    xh, core = lax.div(filt, 2), lax.rem(filt, 2)
    sib = (seq, xh * 2 + 1 - core)
    up = (q * 8 + lax.rem(z + 1, 8), filt)
    down = (q * 8 + lax.rem(z + 7, 8), filt)

    def plane(dx, dq):
        return (lax.rem(q + dq, 8) * 8 + z, lax.rem(xh + dx, 2) * 2 + core)

    def remote(src, dst, send, recv, to):
        return pltpu.make_async_remote_copy(
            src_ref=src, dst_ref=dst, send_sem=send, recv_sem=recv,
            device_id=to, device_id_type=MESH,
        )

    sent = []

    def go(copy):
        copy.start()
        sent.append(copy)

    def near(dz, dq):
        return (lax.rem(q + dq, 8) * 8 + lax.rem(z + dz + 8, 8), filt)

    barrier = pltpu.get_barrier_semaphore()
    partners = (
        [sib]
        + [plane(r // 8, r % 8) for r in range(1, 16)]
        + [near(dz, r) for dz in (1, -1) for r in range(8)]
    )
    for to in partners:
        pl.semaphore_signal(barrier, inc=1, device_id=to, device_id_type=MESH)

    rows = pl.ds(pl.multiple_of(core * 64, 64), 64)
    lanes = pl.ds(pl.multiple_of(q * B, B), B)
    f_in = pltpu.make_async_copy(f_ref, fv, loc.at[4])
    g_own = pltpu.make_async_copy(g_ref.at[rows, lanes], gl.at[0, core, q], loc.at[6])
    g_in = pltpu.make_async_copy(g_ref.at[rows], gv, loc.at[5])
    x_in = pltpu.make_async_copy(x_ref, xv, loc.at[7])
    p_copies = [
        pltpu.make_async_copy(p_ref.at[k, :, lanes], pn.at[:, pl.ds(k * B, B)], loc.at[k])
        for k in range(3)
    ]
    for c in [g_in, g_own, f_in, x_in] + p_copies:
        c.start()
    f_in.wait()
    pick = jnp.where(
        lax.broadcasted_iota(jnp.int32, (8, 12), 1)
        == lax.broadcasted_iota(jnp.int32, (8, 12), 0) + 3 * filt,
        1.0, 0.0,
    ).astype(BF16)
    taps[:, 0:B] = jnp.zeros((8, B), F32)
    taps[:, B:] = jnp.dot(pick, fv[...], preferred_element_type=F32)
    g2[0, 1024:1152, 0:B] = jnp.zeros((B, B), BF16)
    g2[0, 896:1152, B:2 * B] = jnp.zeros((2 * B, B), BF16)

    def build(j, carry):
        for i in range(8):
            upper = lax.broadcasted_iota(jnp.int32, (16, B), 1) >= (
                lax.broadcasted_iota(jnp.int32, (16, B), 0) + 16 * i
            )
            for k in range(3):
                before = None
                for d in range(-1, 8):
                    row = taps[k:k + 1, pl.ds(pl.multiple_of((8 * j + d + 1) * B, B), B)]
                    turned = pltpu.roll(
                        jnp.broadcast_to(row, (16, B)), 16 * i, 1, stride=1, stride_axis=0
                    )
                    if d >= 0:
                        hank[d, k * B + 16 * i:k * B + 16 * i + 16,
                             pl.ds(pl.multiple_of(j * B, B), B)] = jnp.where(
                                 upper, turned, before
                             ).astype(BF16)
                    before = turned
        return carry

    lax.fori_loop(0, 4, build, 0)
    g_in.wait()
    g_own.wait()

    pl.semaphore_wait(barrier, len(partners))

    a2a = []
    for r in range(1, 8):
        col = pl.ds(pl.multiple_of(lax.rem(q + r, 8) * B, B), B)
        a2a.append(
            remote(gv.at[:, col], gl.at[0, core, q], ga_s.at[r], ga_r.at[r], plane(0, r))
        )
        go(a2a[-1])
    lax.fori_loop(4, 8, build, 0)

    x_in.wait()
    for t in range(8):
        flip = xv[:, t * B:(t + 1) * B].T
        for zz in range(8):
            xs[zz, t * 16:(t + 1) * 16, :] = flip[zz * 16:(zz + 1) * 16]
    half = pl.ds(core * 4, 4)
    x_own = pltpu.make_async_copy(xs.at[half], xt.at[half, :, lanes], loc.at[3])
    x_own.start()

    def sub(slot, s):
        return gl.at[slot, core, pl.ds(s * 2, 2)]

    def ring_send(step, s, way):
        here = -step % 8 if way == 0 else step
        there = (-step - 1) % 8 if way == 0 else step + 1
        return remote(
            sub(here, s), sub(there, s),
            gr_s.at[way, step, s], gr_r.at[way, step, s], up if way == 0 else down,
        )

    def hand_over(slot):
        mine = gl.at[slot, core]
        return remote(mine, mine, gs_s.at[slot], gs_r.at[slot], sib)

    def handed(slot):
        other = gl.at[slot, 1 - core]
        return remote(other, other, gs_s.at[slot], gs_r.at[slot], sib)

    for c in a2a:
        c.wait_recv()
    for s in range(4):
        for way in range(2):
            go(ring_send(0, s, way))
    go(hand_over(0))

    x_sends = []
    for r in range(1, 8):
        x_sends.append(
            remote(xs.at[half], xt.at[half, :, lanes], xa_s.at[r], xa_r.at[r], plane(0, r))
        )
        go(x_sends[-1])

    def conv(o):
        slot = o % 8
        if o == 4:
            for s in range(4):
                other = gl.at[4, 1 - core, pl.ds(s * 2, 2)]
                remote(other, other, ge_s.at[s], ge_r.at[s], sib).wait_recv()
        else:
            handed(slot).wait_recv()
        buf = g2.at[0]
        for m in range(8):
            for h in range(2):
                piece = gl[slot, h, m]
                buf[m * B + h * 64:m * B + h * 64 + 64, 0:B] = piece
                if m > 0:
                    buf[(m - 1) * B + h * 64:(m - 1) * B + h * 64 + 64, B:2 * B] = piece
        wrap = jnp.where(lax.rem(z + o + 8, 8) < z, 1, 0)
        for p in range(4):
            depth = B * (8 - 2 * p)
            start = pl.multiple_of(wrap * B + 2 * p * B, B)
            term = jnp.dot(
                hank[slot, :, 0:depth], buf[pl.ds(start, depth), :],
                preferred_element_type=F32,
            )
            if o == 0:
                acc[p] = term
            elif o != 4:
                acc[p] += term
            else:
                done = (acc[p] + term).astype(BF16)
                for e in range(2):
                    for k in range(3):
                        corr[(2 * p + e) * B:(2 * p + e + 1) * B, k * B:(k + 1) * B] = done[
                            k * B:(k + 1) * B, e * B:(e + 1) * B
                        ]

    conv(0)
    for step in range(1, 4):
        for s in range(4):
            for way in range(2):
                ring_send(step - 1, s, way).wait_recv()
                if step < 3 or s // 2 == way:
                    go(ring_send(step, s, way))
        go(hand_over(-step % 8))
        go(hand_over(step))
        if step > 1:
            conv(step - 1)
            conv(1 - step)
        if step == 3:
            x_own.wait()
            for c in x_sends:
                c.wait_recv()
            x_hand = remote(xt.at[half], xt.at[half], xs_s, xs_r, sib)
            go(x_hand)
    conv(3)
    for s in range(4):
        ring_send(3, s, s // 2).wait_recv()
        mine = sub(4, s)
        go(remote(mine, mine, ge_s.at[s], ge_r.at[s], sib))
    conv(-3)
    conv(4)

    for p in p_copies:
        p.wait()

    def tile(x_to, of_core, upper_half):
        cols = pl.ds(pl.multiple_of(x_to * 512 + of_core * 256, 256), 256)
        return lax.dot_general(
            corr[pl.ds(pl.multiple_of(upper_half * 512, 512), 512), :], pn[cols, :],
            (((1,), (1,)), ((), ())), preferred_element_type=F32,
        ).reshape(4, B, 256)

    def across(dx, du, dm):
        m = lax.rem(lax.div(q, 4) + du, 2) * 4 + lax.rem(lax.rem(q, 4) + dm, 4)
        return lax.rem(xh + dx, 2), m

    quarters = []
    for dx, du in ((1, 1), (1, 0), (0, 1), (0, 0)):
        x_to, u = lax.rem(xh + dx, 2), lax.rem(lax.div(q, 4) + du, 2)
        quarters.append((dx, du, x_to, u, pl.ds(u * 4, 4)))
    swaps = []
    for n, (dx, du, x_to, u, part) in enumerate(quarters):
        igs[x_to, part] = tile(x_to, 1 - core, u).astype(BF16)
        swaps.append(
            remote(igs.at[x_to, part], igr.at[x_to, part], is_s.at[n], is_r.at[n], sib)
        )
        go(swaps[-1])

    half_o = pl.ds((1 - core) * 4, 4)
    remote(xt.at[half_o], xt.at[half_o], xs_s, xs_r, sib).wait_recv()

    def at(o):
        return lax.rem(z + o + 8, 8)

    def products(*offsets):
        for o in offsets:
            part = jnp.dot(xt[at(o)], corr[...], preferred_element_type=F32).astype(BF16)
            for k in range(3):
                if o == 0:
                    pgo[:, k] = part[:, k * B:(k + 1) * B].reshape(8, 16, B)
                else:
                    pgb[at(o), k] = part[:, k * B:(k + 1) * B]

    def sum_send(step, k, way):
        src = pgb.at[at(4 if way == 0 else -3), k] if step == 0 else pgs.at[way, step - 1, k]
        return remote(
            src, pgr.at[way, step, k], pr_s.at[way, step, k], pr_r.at[way, step, k],
            up if way == 0 else down,
        )

    def sum_step(step, k, way):
        last = step == (3 if way == 0 else 2)
        o = 4 - step if way == 0 else step - 3
        sum_send(step - 1, k, way).wait_recv()
        total = (
            pgr[way, step - 1, k].astype(F32) + pgb[at(o), k].astype(F32)
        ).astype(BF16)
        if last:
            pga[way, :, k] = total.reshape(8, 16, B)
        else:
            pgs[way, step - 1, k] = total
            go(sum_send(step, k, way))
        if last and k == 2:
            for r in range(8):
                go(remote(
                    pga.at[way, lax.rem(q + r, 8)], pgp.at[way + 1, q],
                    pa_s.at[way + 1, r], pa_r.at[way + 1, q], near(1 if way == 0 else -1, r),
                ))

    products(4, -3)
    for k in range(3):
        for way in range(2):
            go(sum_send(0, k, way))
    products(3, -2)
    for dx, du, x_to, u, part in quarters:
        igo[x_to, part] = tile(x_to, core, u)

    ig_sends = []

    def quarter(n):
        dx, du, x_to, u, part = quarters[n]
        swaps[n].wait_recv()
        igc[x_to, part] = (igo[x_to, part] + igr[x_to, part].astype(F32)).astype(BF16)
        for dm in range(4):
            if dx + du + dm == 0:
                continue
            r = dx * 8 + du * 4 + dm
            to_x, to_m = across(dx, du, dm)
            ig_sends.append((r, remote(
                igc.at[to_x, to_m], igd.at[r], id_s.at[r], id_r.at[r],
                (to_m * 8 + z, to_x * 2 + core),
            )))
            go(ig_sends[-1][1])

    for n in range(4):
        quarter(n)
    for k in range(3):
        for way in range(2):
            sum_step(1, k, way)
    products(2, -1, 1, 0)
    pg_sends = []
    for r in range(1, 8):
        pg_sends.append(
            remote(
                pgo.at[lax.rem(q + r, 8)], pgp.at[0, q], pa_s.at[0, r], pa_r.at[0, r],
                plane(0, r),
            )
        )
        go(pg_sends[-1])
    pgp[0, q] = pgo[q]
    for k in range(3):
        for way in range(2):
            sum_step(2, k, way)
    for k in range(3):
        sum_step(3, k, 0)

    total = igc[xh, q].astype(F32)
    for r, c in ig_sends:
        c.wait_recv()
        total = total + igd[r].astype(F32)
    ig_ref[...] = total.astype(BF16)

    for c in pg_sends:
        c.wait_recv()
    for s in range(8):
        for d in (1, 2):
            here = pgp.at[d, s]
            remote(here, here, pa_s.at[d, 0], pa_r.at[d, s], up).wait_recv()
        total = (
            pgp[0, s].astype(F32) + pgp[1, s].astype(F32) + pgp[2, s].astype(F32)
        ) * (8192.0 ** -0.5)
        pg_ref[:, :, s * B:(s + 1) * B] = total.astype(BF16)
    for c in sent:
        c.wait_send()


def per_device(inputs, cotangent, filters, projections):
    vmem = pl.BlockSpec(memory_space=pltpu.VMEM)
    dma = pltpu.SemaphoreType.DMA
    return pl.pallas_call(
        kernel,
        out_shape=(
            jax.ShapeDtypeStruct((B, 256), BF16),
            jax.ShapeDtypeStruct((3, 16, 1024), BF16),
        ),
        in_specs=[pl.BlockSpec(memory_space=pl.ANY)] * 4,
        out_specs=(vmem, vmem),
        scratch_shapes=[
            pltpu.VMEM((8, 8192 + B), F32),
            pltpu.VMEM((12, 8192), BF16),
            pltpu.VMEM((64, 1024), BF16),
            pltpu.VMEM((B, 1024), BF16),
            pltpu.VMEM((8, 384, 1024), BF16),
            pltpu.VMEM((8, 2, 8, 64, B), BF16),
            pltpu.VMEM((1, 1152, 256), BF16),
            pltpu.VMEM((4, 384, 256), F32),
            pltpu.VMEM((1024, 384), BF16),
            pltpu.VMEM((8, B, B), BF16),
            pltpu.VMEM((8, B, 1024), BF16),
            pltpu.VMEM((1024, 384), BF16),
            pltpu.VMEM((8, 3, B, B), BF16),
            pltpu.VMEM((2, 4, 3, B, B), BF16),
            pltpu.VMEM((2, 2, 3, B, B), BF16),
            pltpu.VMEM((2, 8, 3, 16, B), BF16),
            pltpu.VMEM((8, 3, 16, B), BF16),
            pltpu.VMEM((3, 8, 3, 16, B), BF16),
            pltpu.VMEM((2, 8, B, 256), BF16),
            pltpu.VMEM((2, 8, B, 256), BF16),
            pltpu.VMEM((2, 8, B, 256), F32),
            pltpu.VMEM((2, 8, B, 256), BF16),
            pltpu.VMEM((16, B, 256), BF16),
            dma((8,)), dma((8,)),
            dma((2, 4, 4)), dma((2, 4, 4)),
            dma((8,)), dma((8,)),
            dma((4,)), dma((4,)),
            dma((8,)), dma((8,)),
            dma, dma,
            dma((8,)),
            dma((2, 4, 3)), dma((2, 4, 3)),
            dma((3, 8)), dma((3, 8)),
            dma((4,)), dma((4,)),
            dma((16,)), dma((16,)),
        ],
        compiler_params=pltpu.CompilerParams(
            collective_id=0, has_side_effects=True, vmem_limit_bytes=48 * 1024 * 1024
        ),
        cost_estimate=pl.CostEstimate(
            flops=6_000_000_000, bytes_accessed=2_000_000, transcendentals=0
        ),
    )(*(
        pltpu.with_memory_space_constraint(a, pltpu.HBM)
        for a in (inputs, cotangent, filters, projections)
    ))


def solution(mesh):
    placed = (P("seq", None), P("seq", None), P(), P("filt", None, None))
    return jax.shard_map(
        per_device,
        mesh=mesh,
        in_specs=placed,
        out_specs=(P("seq", "filt"), P("filt", "seq", None)),
        check_vma=False,
    )
```

```python
import functools

import jax
import jax.numpy as jnp
from jax import lax
from jax.experimental import pallas as pl
from jax.experimental.pallas import tpu as pltpu
from jax.sharding import PartitionSpec as P

MESH = pl.DeviceIdType.MESH
F32 = jnp.float32
BF16 = jnp.bfloat16
B = 128
ORDER = (0, 1, -1, 2, -2, 3, -3, 4)


def kernel(
    x_ref, g_ref, f_ref, p_ref, ig_ref, pg_ref,
    taps, fv, gv, xv, hank, gl, g2, acc, corr, xs, xt, pn, pgb, pgr, pgs, pga, pgo, pgp,
    iga, igb, ra, rb, igt, fa, fb,
    ga_s, ga_r, gr_s, gr_r, gs_s, gs_r, ge_s, ge_r, xa_s, xa_r, xs_s, xs_r, loc,
    pr_s, pr_r, pa_s, pa_r, pp_s, pp_r, cs_s, cs_r, ip_s, ip_r, iq_s, iq_r,
):
    seq = lax.axis_index("seq")
    filt = lax.axis_index("filt")
    q, z = lax.div(seq, 8), lax.rem(seq, 8)
    xh, core = lax.div(filt, 2), lax.rem(filt, 2)
    x, y = xh * 2 + lax.rem(q, 2), lax.div(q, 2)
    sib = (seq, xh * 2 + 1 - core)
    up = (q * 8 + lax.rem(z + 1, 8), filt)
    down = (q * 8 + lax.rem(z + 7, 8), filt)

    def plane(dx, dq):
        return (lax.rem(q + dq, 8) * 8 + z, lax.rem(xh + dx, 2) * 2 + core)

    def remote(src, dst, send, recv, to):
        return pltpu.make_async_remote_copy(
            src_ref=src, dst_ref=dst, send_sem=send, recv_sem=recv,
            device_id=to, device_id_type=MESH,
        )

    sent = []

    def go(copy):
        copy.start()
        sent.append(copy)

    def chip(dx, dy):
        to_x, to_y = lax.rem(x + dx, 4), lax.rem(y + dy, 4)
        return ((to_y * 2 + lax.rem(to_x, 2)) * 8 + z, lax.div(to_x, 2) * 2 + core)

    def near(dz, dq):
        return (lax.rem(q + dq, 8) * 8 + lax.rem(z + dz + 8, 8), filt)

    barrier = pltpu.get_barrier_semaphore()
    partners = (
        [sib]
        + [plane(0, r) for r in range(1, 8)]
        + [((y * 2 + side) * 8 + z, (1 - xh) * 2 + core) for side in range(2)]
        + [near(dz, r) for dz in (1, -1) for r in range(8)]
    )
    for to in partners:
        pl.semaphore_signal(barrier, inc=1, device_id=to, device_id_type=MESH)

    rows = pl.ds(pl.multiple_of(core * 64, 64), 64)
    lanes = pl.ds(pl.multiple_of(q * B, B), B)
    own = pl.ds(pl.multiple_of(core * 384, 128), 384)

    def p_slice(k, to, of_core):
        e = pl.ds(pl.multiple_of(to * 512 + of_core * 256, 256), 256)
        return p_ref.at[k, e, lanes]

    def p_place(k, to):
        return pn.at[to, :, pl.ds(pl.multiple_of(core * 384 + k * B, B), B)]

    f_in = pltpu.make_async_copy(f_ref, fv, loc.at[4])
    g_own = pltpu.make_async_copy(g_ref.at[rows, lanes], gl.at[0, core, q], loc.at[6])
    g_in = pltpu.make_async_copy(g_ref.at[rows], gv, loc.at[5])
    x_in = pltpu.make_async_copy(x_ref, xv, loc.at[7])
    p_copies = [
        pltpu.make_async_copy(p_slice(k, to, core), p_place(k, to), loc.at[8 + 2 * k + to])
        for k in range(3)
        for to in range(2)
    ]
    for c in [g_in, g_own, f_in, x_in] + p_copies:
        c.start()
    f_in.wait()
    pick = jnp.where(
        lax.broadcasted_iota(jnp.int32, (8, 12), 1)
        == lax.broadcasted_iota(jnp.int32, (8, 12), 0) + 3 * filt,
        1.0, 0.0,
    ).astype(BF16)
    taps[:, 0:B] = jnp.zeros((8, B), F32)
    taps[:, B:] = jnp.dot(pick, fv[...], preferred_element_type=F32)
    g2[0, 1024:1152, 0:B] = jnp.zeros((B, B), BF16)
    g2[0, 896:1152, B:2 * B] = jnp.zeros((2 * B, B), BF16)

    def build(j, carry):
        for i in range(8):
            upper = lax.broadcasted_iota(jnp.int32, (16, B), 1) >= (
                lax.broadcasted_iota(jnp.int32, (16, B), 0) + 16 * i
            )
            for k in range(3):
                before = None
                for d in range(-1, 8):
                    row = taps[k:k + 1, pl.ds(pl.multiple_of((8 * j + d + 1) * B, B), B)]
                    turned = pltpu.roll(
                        jnp.broadcast_to(row, (16, B)), 16 * i, 1, stride=1, stride_axis=0
                    )
                    if d >= 0:
                        hank[d, k * B + 16 * i:k * B + 16 * i + 16,
                             pl.ds(pl.multiple_of(j * B, B), B)] = jnp.where(
                                 upper, turned, before
                             ).astype(BF16)
                    before = turned
        return carry

    lax.fori_loop(0, 4, build, 0)
    g_in.wait()
    g_own.wait()

    pl.semaphore_wait(barrier, len(partners))

    a2a = []
    for r in range(1, 8):
        col = pl.ds(pl.multiple_of(lax.rem(q + r, 8) * B, B), B)
        a2a.append(
            remote(gv.at[:, col], gl.at[0, core, q], ga_s.at[r], ga_r.at[r], plane(0, r))
        )
        go(a2a[-1])
    p_sends = [
        remote(
            p_slice(k, to, 1 - core), p_place(k, to), pp_s.at[2 * k + to], pp_r.at[2 * k + to], sib
        )
        for k in range(3)
        for to in range(2)
    ]
    for c in p_sends:
        go(c)
    lax.fori_loop(4, 8, build, 0)

    x_in.wait()
    for t in range(8):
        flip = xv[:, t * B:(t + 1) * B].T
        for zz in range(8):
            xs[zz, t * 16:(t + 1) * 16, :] = flip[zz * 16:(zz + 1) * 16]
    half = pl.ds(core * 4, 4)
    x_own = pltpu.make_async_copy(xs.at[half], xt.at[half, :, lanes], loc.at[3])
    x_own.start()

    def sub(slot, s):
        return gl.at[slot, core, pl.ds(s * 2, 2)]

    def ring_send(step, s, way):
        here = -step % 8 if way == 0 else step
        there = (-step - 1) % 8 if way == 0 else step + 1
        return remote(
            sub(here, s), sub(there, s),
            gr_s.at[way, step, s], gr_r.at[way, step, s], up if way == 0 else down,
        )

    def hand_over(slot):
        mine = gl.at[slot, core]
        return remote(mine, mine, gs_s.at[slot], gs_r.at[slot], sib)

    def handed(slot):
        other = gl.at[slot, 1 - core]
        return remote(other, other, gs_s.at[slot], gs_r.at[slot], sib)

    for c in a2a:
        c.wait_recv()
    for s in range(4):
        for way in range(2):
            go(ring_send(0, s, way))
    go(hand_over(0))

    x_sends = []
    for r in range(1, 8):
        x_sends.append(
            remote(xs.at[half], xt.at[half, :, lanes], xa_s.at[r], xa_r.at[r], plane(0, r))
        )
        go(x_sends[-1])

    corr_sends = []

    def conv(o):
        slot = o % 8
        if o == 4:
            for s in range(4):
                other = gl.at[4, 1 - core, pl.ds(s * 2, 2)]
                remote(other, other, ge_s.at[s], ge_r.at[s], sib).wait_recv()
        else:
            handed(slot).wait_recv()
        buf = g2.at[0]
        for m in range(8):
            for h in range(2):
                piece = gl[slot, h, m]
                buf[m * B + h * 64:m * B + h * 64 + 64, 0:B] = piece
                if m > 0:
                    buf[(m - 1) * B + h * 64:(m - 1) * B + h * 64 + 64, B:2 * B] = piece
        wrap = jnp.where(lax.rem(z + o + 8, 8) < z, 1, 0)
        for p in range(4):
            depth = B * (8 - 2 * p)
            start = pl.multiple_of(wrap * B + 2 * p * B, B)
            term = jnp.dot(
                hank[slot, :, 0:depth], buf[pl.ds(start, depth), :],
                preferred_element_type=F32,
            )
            if o == 0:
                acc[p] = term
            elif o != 4:
                acc[p] += term
            else:
                done = (acc[p] + term).astype(BF16)
                for e in range(2):
                    for k in range(3):
                        corr[
                            (2 * p + e) * B:(2 * p + e + 1) * B,
                            pl.ds(pl.multiple_of(core * 384 + k * B, B), B),
                        ] = done[k * B:(k + 1) * B, e * B:(e + 1) * B]
                mine = corr.at[pl.ds(p * 256, 256), own]
                corr_sends.append(remote(mine, mine, cs_s.at[p], cs_r.at[p], sib))
                go(corr_sends[-1])

    conv(0)
    for step in range(1, 4):
        for s in range(4):
            for way in range(2):
                ring_send(step - 1, s, way).wait_recv()
                if step < 3 or s // 2 == way:
                    go(ring_send(step, s, way))
        go(hand_over(-step % 8))
        go(hand_over(step))
        if step > 1:
            conv(step - 1)
            conv(1 - step)
        if step == 3:
            x_own.wait()
            for c in x_sends:
                c.wait_recv()
            x_hand = remote(xt.at[half], xt.at[half], xs_s, xs_r, sib)
            go(x_hand)
    conv(3)
    for s in range(4):
        ring_send(3, s, s // 2).wait_recv()
        mine = sub(4, s)
        go(remote(mine, mine, ge_s.at[s], ge_r.at[s], sib))
    conv(-3)
    conv(4)

    half_o = pl.ds((1 - core) * 4, 4)
    remote(xt.at[half_o], xt.at[half_o], xs_s, xs_r, sib).wait_recv()

    def at(o):
        return lax.rem(z + o + 8, 8)

    def products(*offsets):
        for o in offsets:
            part = jnp.dot(xt[at(o)], corr[:, own], preferred_element_type=F32).astype(BF16)
            for k in range(3):
                if o == 0:
                    pgo[:, k] = part[:, k * B:(k + 1) * B].reshape(8, 16, B)
                else:
                    pgb[at(o), k] = part[:, k * B:(k + 1) * B]

    def sum_send(step, k, way):
        src = pgb.at[at(4 if way == 0 else -3), k] if step == 0 else pgs.at[way, step - 1, k]
        return remote(
            src, pgr.at[way, step, k], pr_s.at[way, step, k], pr_r.at[way, step, k],
            up if way == 0 else down,
        )

    def sum_step(step, k, way):
        last = step == (3 if way == 0 else 2)
        o = 4 - step if way == 0 else step - 3
        sum_send(step - 1, k, way).wait_recv()
        total = (
            pgr[way, step - 1, k].astype(F32) + pgb[at(o), k].astype(F32)
        ).astype(BF16)
        if last:
            pga[way, :, k] = total.reshape(8, 16, B)
        else:
            pgs[way, step - 1, k] = total
            go(sum_send(step, k, way))
        if last and k == 2:
            for r in range(8):
                go(remote(
                    pga.at[way, lax.rem(q + r, 8)], pgp.at[way + 1, q],
                    pa_s.at[way + 1, r], pa_r.at[way + 1, q], near(1 if way == 0 else -1, r),
                ))

    products(4, -3)
    for k in range(3):
        for way in range(2):
            go(sum_send(0, k, way))

    for c in p_copies:
        c.wait()
    for c in p_sends:
        c.wait_recv()
    for c in corr_sends:
        c.wait_recv()
    ig_sends = []
    for dy in (2, 1, 3, 0):
        pair = lax.rem(y + dy, 4)
        rows_of = corr[pl.ds(pl.multiple_of(pair * 256, 256), 256), :]
        for to in range(2):
            part = lax.dot_general(
                rows_of, pn[to], (((1,), (1,)), ((), ())), preferred_element_type=F32
            ).astype(BF16)
            for side in range(2):
                iga[2 * to + side, pair] = part[side * B:(side + 1) * B, 0:B]
                igb[pair, 2 * to + side] = part[side * B:(side + 1) * B, B:2 * B]
        if dy:
            ig_sends.append(remote(
                igb.at[pair], rb.at[dy], ip_s.at[1, dy], ip_r.at[1, dy], chip(0, dy)
            ))
            go(ig_sends[-1])
    for dx in (2, 1, 3):
        ig_sends.append(remote(
            iga.at[lax.rem(x + dx, 4)], ra.at[dx], ip_s.at[0, dx], ip_r.at[0, dx], chip(dx, 0)
        ))
        go(ig_sends[-1])

    products(3, -2)
    for k in range(3):
        for way in range(2):
            sum_step(1, k, way)
    products(2, -1, 1, 0)
    pg_sends = []
    for r in range(1, 8):
        pg_sends.append(
            remote(
                pgo.at[lax.rem(q + r, 8)], pgp.at[0, q], pa_s.at[0, r], pa_r.at[0, r],
                plane(0, r),
            )
        )
        go(pg_sends[-1])
    pgp[0, q] = pgo[q]
    for k in range(3):
        for way in range(2):
            sum_step(2, k, way)

    for c in ig_sends:
        c.wait_recv()
    ig_last = []
    for d in (2, 1, 3):
        for mine, got, last, n in ((iga.at[x], ra, fa, 0), (igb.at[y], rb, fb, 1)):
            there = lax.rem((y if n == 0 else x) + d, 4)
            total = mine[there].astype(F32)
            for e in range(1, 4):
                total = total + got[e, there].astype(F32)
            out = igt.at[n, d]
            out[...] = total.astype(BF16)
            ig_last.append(remote(
                out, last.at[d], iq_s.at[n, d], iq_r.at[n, d],
                chip(0, d) if n == 0 else chip(d, 0),
            ))
            go(ig_last[-1])
    for k in range(3):
        sum_step(3, k, 0)

    halves = []
    for mine, got, here in ((iga.at[x], ra, y), (igb.at[y], rb, x)):
        total = mine[here].astype(F32)
        for e in range(1, 4):
            total = total + got[e, here].astype(F32)
        halves.append(total)
    for c in ig_last:
        c.wait_recv()
    for n, last in ((0, fa), (1, fb)):
        total = halves[n]
        for e in range(1, 4):
            total = total + last[e].astype(F32)
        ig_ref[:, n * B:(n + 1) * B] = total.astype(BF16)

    for c in pg_sends:
        c.wait_recv()
    for s in range(8):
        for d in (1, 2):
            here = pgp.at[d, s]
            remote(here, here, pa_s.at[d, 0], pa_r.at[d, s], up).wait_recv()
        total = (
            pgp[0, s].astype(F32) + pgp[1, s].astype(F32) + pgp[2, s].astype(F32)
        ) * (8192.0 ** -0.5)
        pg_ref[:, :, s * B:(s + 1) * B] = total.astype(BF16)
    for c in sent:
        c.wait_send()


def per_device(inputs, cotangent, filters, projections):
    vmem = pl.BlockSpec(memory_space=pltpu.VMEM)
    dma = pltpu.SemaphoreType.DMA
    return pl.pallas_call(
        kernel,
        out_shape=(
            jax.ShapeDtypeStruct((B, 256), BF16),
            jax.ShapeDtypeStruct((3, 16, 1024), BF16),
        ),
        in_specs=[pl.BlockSpec(memory_space=pl.ANY)] * 4,
        out_specs=(vmem, vmem),
        scratch_shapes=[
            pltpu.VMEM((8, 8192 + B), F32),
            pltpu.VMEM((12, 8192), BF16),
            pltpu.VMEM((64, 1024), BF16),
            pltpu.VMEM((B, 1024), BF16),
            pltpu.VMEM((8, 384, 1024), BF16),
            pltpu.VMEM((8, 2, 8, 64, B), BF16),
            pltpu.VMEM((1, 1152, 256), BF16),
            pltpu.VMEM((4, 384, 256), F32),
            pltpu.VMEM((1024, 768), BF16),
            pltpu.VMEM((8, B, B), BF16),
            pltpu.VMEM((8, B, 1024), BF16),
            pltpu.VMEM((2, 256, 768), BF16),
            pltpu.VMEM((8, 3, B, B), BF16),
            pltpu.VMEM((2, 4, 3, B, B), BF16),
            pltpu.VMEM((2, 2, 3, B, B), BF16),
            pltpu.VMEM((2, 8, 3, 16, B), BF16),
            pltpu.VMEM((8, 3, 16, B), BF16),
            pltpu.VMEM((3, 8, 3, 16, B), BF16),
            pltpu.VMEM((4, 4, B, B), BF16),
            pltpu.VMEM((4, 4, B, B), BF16),
            pltpu.VMEM((4, 4, B, B), BF16),
            pltpu.VMEM((4, 4, B, B), BF16),
            pltpu.VMEM((2, 4, B, B), BF16),
            pltpu.VMEM((4, B, B), BF16),
            pltpu.VMEM((4, B, B), BF16),
            dma((8,)), dma((8,)),
            dma((2, 4, 4)), dma((2, 4, 4)),
            dma((8,)), dma((8,)),
            dma((4,)), dma((4,)),
            dma((8,)), dma((8,)),
            dma, dma,
            dma((14,)),
            dma((2, 4, 3)), dma((2, 4, 3)),
            dma((3, 8)), dma((3, 8)),
            dma((6,)), dma((6,)),
            dma((4,)), dma((4,)),
            dma((2, 4)), dma((2, 4)),
            dma((2, 4)), dma((2, 4)),
        ],
        compiler_params=pltpu.CompilerParams(
            collective_id=0, has_side_effects=True, vmem_limit_bytes=48 * 1024 * 1024
        ),
        cost_estimate=pl.CostEstimate(
            flops=6_000_000_000, bytes_accessed=2_000_000, transcendentals=0
        ),
    )(*(
        pltpu.with_memory_space_constraint(a, pltpu.HBM)
        for a in (inputs, cotangent, filters, projections)
    ))


def solution(mesh):
    placed = (P("seq", None), P("seq", None), P(), P("filt", None, None))
    return jax.shard_map(
        per_device,
        mesh=mesh,
        in_specs=placed,
        out_specs=(P("seq", "filt"), P("filt", "seq", None)),
        check_vma=False,
    )
```

```python
import functools

import jax
import jax.numpy as jnp
from jax import lax
from jax.experimental import pallas as pl
from jax.experimental.pallas import tpu as pltpu
from jax.sharding import PartitionSpec as P

MESH = pl.DeviceIdType.MESH
F32 = jnp.float32
BF16 = jnp.bfloat16
B = 128
ORDER = (0, 1, -1, 2, -2, 3, -3, 4)


def kernel(
    x_ref, g_ref, f_ref, p_ref, ig_ref, pg_ref,
    taps, fv, gv, xv, hank, gl, g2, acc, corr, xs, xt, pn, pgb, pgr, pgh, pgs, pga, pgo, pgp,
    iga, igb, ra, rb, igt, fa, fb,
    ga_s, ga_r, gr_s, gr_r, gs_s, gs_r, ge_s, ge_r, xa_s, xa_r, xs_s, xs_r, loc,
    pr_s, pr_r, ph_s, ph_r, pa_s, pa_r, pp_s, pp_r, cs_s, cs_r, ip_s, ip_r, iq_s, iq_r,
):
    seq = lax.axis_index("seq")
    filt = lax.axis_index("filt")
    q, z = lax.div(seq, 8), lax.rem(seq, 8)
    xh, core = lax.div(filt, 2), lax.rem(filt, 2)
    x, y = xh * 2 + lax.rem(q, 2), lax.div(q, 2)
    sib = (seq, xh * 2 + 1 - core)
    up = (q * 8 + lax.rem(z + 1, 8), filt)
    down = (q * 8 + lax.rem(z + 7, 8), filt)

    def plane(dx, dq):
        return (lax.rem(q + dq, 8) * 8 + z, lax.rem(xh + dx, 2) * 2 + core)

    def remote(src, dst, send, recv, to):
        return pltpu.make_async_remote_copy(
            src_ref=src, dst_ref=dst, send_sem=send, recv_sem=recv,
            device_id=to, device_id_type=MESH,
        )

    sent = []

    def go(copy):
        copy.start()
        sent.append(copy)

    def chip(dx, dy):
        to_x, to_y = lax.rem(x + dx, 4), lax.rem(y + dy, 4)
        return ((to_y * 2 + lax.rem(to_x, 2)) * 8 + z, lax.div(to_x, 2) * 2 + core)

    def near(dz, dq):
        return (lax.rem(q + dq, 8) * 8 + lax.rem(z + dz + 8, 8), filt)

    barrier = pltpu.get_barrier_semaphore()
    partners = (
        [sib]
        + [plane(0, r) for r in range(1, 8)]
        + [((y * 2 + side) * 8 + z, (1 - xh) * 2 + core) for side in range(2)]
        + [near(dz, r) for dz in (1, -1) for r in range(8)]
        + [near(2, 0), near(-2, 0)]
    )
    for to in partners:
        pl.semaphore_signal(barrier, inc=1, device_id=to, device_id_type=MESH)

    rows = pl.ds(pl.multiple_of(core * 64, 64), 64)
    lanes = pl.ds(pl.multiple_of(q * B, B), B)
    own = pl.ds(pl.multiple_of(core * 384, 128), 384)

    def p_slice(k, to, of_core):
        e = pl.ds(pl.multiple_of(to * 512 + of_core * 256, 256), 256)
        return p_ref.at[k, e, lanes]

    def p_place(k, to):
        return pn.at[to, :, pl.ds(pl.multiple_of(core * 384 + k * B, B), B)]

    f_in = pltpu.make_async_copy(f_ref, fv, loc.at[4])
    g_own = pltpu.make_async_copy(g_ref.at[rows, lanes], gl.at[0, core, q], loc.at[6])
    g_in = pltpu.make_async_copy(g_ref.at[rows], gv, loc.at[5])
    x_in = pltpu.make_async_copy(x_ref, xv, loc.at[7])
    p_copies = [
        pltpu.make_async_copy(p_slice(k, to, core), p_place(k, to), loc.at[8 + 2 * k + to])
        for k in range(3)
        for to in range(2)
    ]
    for c in [g_in, g_own, f_in, x_in] + p_copies:
        c.start()
    f_in.wait()
    pick = jnp.where(
        lax.broadcasted_iota(jnp.int32, (8, 12), 1)
        == lax.broadcasted_iota(jnp.int32, (8, 12), 0) + 3 * filt,
        1.0, 0.0,
    ).astype(BF16)
    taps[:, 0:B] = jnp.zeros((8, B), F32)
    taps[:, B:] = jnp.dot(pick, fv[...], preferred_element_type=F32)
    g2[0, 1024:1152, 0:B] = jnp.zeros((B, B), BF16)
    g2[0, 896:1152, B:2 * B] = jnp.zeros((2 * B, B), BF16)

    def build(j, carry):
        for i in range(8):
            upper = lax.broadcasted_iota(jnp.int32, (16, B), 1) >= (
                lax.broadcasted_iota(jnp.int32, (16, B), 0) + 16 * i
            )
            for k in range(3):
                before = None
                for d in range(-1, 8):
                    row = taps[k:k + 1, pl.ds(pl.multiple_of((8 * j + d + 1) * B, B), B)]
                    turned = pltpu.roll(
                        jnp.broadcast_to(row, (16, B)), 16 * i, 1, stride=1, stride_axis=0
                    )
                    if d >= 0:
                        hank[d, k * B + 16 * i:k * B + 16 * i + 16,
                             pl.ds(pl.multiple_of(j * B, B), B)] = jnp.where(
                                 upper, turned, before
                             ).astype(BF16)
                    before = turned
        return carry

    lax.fori_loop(0, 4, build, 0)
    g_in.wait()
    g_own.wait()

    pl.semaphore_wait(barrier, len(partners))

    for n, (dy, side) in enumerate(((2, 1), (2, 0), (1, 1), (3, 1), (1, 0), (3, 0), (0, 1))):
        to_q = lax.rem(y + dy, 4) * 2 + lax.rem(x + side, 2)
        col = pl.ds(pl.multiple_of(to_q * B, B), B)
        go(remote(
            gv.at[:, col], gl.at[0, core, q], ga_s.at[n], ga_r.at[q], (to_q * 8 + z, filt)
        ))
    p_sends = [
        remote(
            p_slice(k, to, 1 - core), p_place(k, to), pp_s.at[2 * k + to], pp_r.at[2 * k + to], sib
        )
        for k in range(3)
        for to in range(2)
    ]
    for c in p_sends:
        go(c)
    lax.fori_loop(4, 8, build, 0)

    x_in.wait()
    for t in range(8):
        flip = xv[:, t * B:(t + 1) * B].T
        for zz in range(8):
            xs[zz, t * 16:(t + 1) * 16, :] = flip[zz * 16:(zz + 1) * 16]
    half = pl.ds(core * 4, 4)
    x_own = pltpu.make_async_copy(xs.at[half], xt.at[half, :, lanes], loc.at[3])
    x_own.start()

    def turn(s):
        return lax.rem(y + (0, 1, 3, 2)[s], 4)

    def sub(slot, s):
        return gl.at[slot, core, pl.ds(turn(s) * 2, 2)]

    def ring_send(step, s, way):
        here = -step % 8 if way == 0 else step
        there = (-step - 1) % 8 if way == 0 else step + 1
        return remote(
            sub(here, s), sub(there, s),
            gr_s.at[way, step, s], gr_r.at[way, step, s], up if way == 0 else down,
        )

    def hand_over(slot):
        mine = gl.at[slot, core]
        return remote(mine, mine, gs_s.at[slot], gs_r.at[slot], sib)

    def handed(slot):
        other = gl.at[slot, 1 - core]
        return remote(other, other, gs_s.at[slot], gs_r.at[slot], sib)

    def landed(from_q):
        here = gl.at[0, core, from_q]
        remote(here, here, ga_s.at[0], ga_r.at[from_q], up).wait_recv()

    landed(lax.div(q, 2) * 2 + lax.rem(q + 1, 2))
    for s in range(4):
        if s:
            landed(turn(s) * 2)
            landed(turn(s) * 2 + 1)
        for way in range(2):
            go(ring_send(0, s, way))
    go(hand_over(0))

    x_sends = []
    for r in range(1, 8):
        x_sends.append(
            remote(xs.at[half], xt.at[half, :, lanes], xa_s.at[r], xa_r.at[r], plane(0, r))
        )
        go(x_sends[-1])

    corr_sends = []

    def conv(o):
        slot = o % 8
        if o == 4:
            for s in range(4):
                other = gl.at[4, 1 - core, pl.ds(turn(s) * 2, 2)]
                remote(other, other, ge_s.at[s], ge_r.at[s], sib).wait_recv()
        else:
            handed(slot).wait_recv()
        buf = g2.at[0]
        for m in range(8):
            for h in range(2):
                piece = gl[slot, h, m]
                buf[m * B + h * 64:m * B + h * 64 + 64, 0:B] = piece
                if m > 0:
                    buf[(m - 1) * B + h * 64:(m - 1) * B + h * 64 + 64, B:2 * B] = piece
        wrap = jnp.where(lax.rem(z + o + 8, 8) < z, 1, 0)
        for p in range(4):
            depth = B * (8 - 2 * p)
            start = pl.multiple_of(wrap * B + 2 * p * B, B)
            term = jnp.dot(
                hank[slot, :, 0:depth], buf[pl.ds(start, depth), :],
                preferred_element_type=F32,
            )
            if o == 0:
                acc[p] = term
            elif o != 4:
                acc[p] += term
            else:
                done = (acc[p] + term).astype(BF16)
                for e in range(2):
                    for k in range(3):
                        corr[
                            (2 * p + e) * B:(2 * p + e + 1) * B,
                            pl.ds(pl.multiple_of(core * 384 + k * B, B), B),
                        ] = done[k * B:(k + 1) * B, e * B:(e + 1) * B]
                mine = corr.at[pl.ds(p * 256, 256), own]
                corr_sends.append(remote(mine, mine, cs_s.at[p], cs_r.at[p], sib))
                go(corr_sends[-1])

    conv(0)
    for step in range(1, 4):
        for s in range(4):
            for way in range(2):
                ring_send(step - 1, s, way).wait_recv()
                if step < 3 or s // 2 == way:
                    go(ring_send(step, s, way))
        go(hand_over(-step % 8))
        go(hand_over(step))
        if step > 1:
            conv(step - 1)
            conv(1 - step)
        if step == 3:
            x_own.wait()
            for c in x_sends:
                c.wait_recv()
            x_hand = remote(xt.at[half], xt.at[half], xs_s, xs_r, sib)
            go(x_hand)
    conv(3)
    for s in range(4):
        ring_send(3, s, s // 2).wait_recv()
        mine = sub(4, s)
        go(remote(mine, mine, ge_s.at[s], ge_r.at[s], sib))
    conv(-3)
    conv(4)

    half_o = pl.ds((1 - core) * 4, 4)
    remote(xt.at[half_o], xt.at[half_o], xs_s, xs_r, sib).wait_recv()

    def at(o):
        return lax.rem(z + o + 8, 8)

    def products(*offsets):
        for o in offsets:
            part = jnp.dot(xt[at(o)], corr[:, own], preferred_element_type=F32).astype(BF16)
            for k in range(3):
                if o == 0:
                    pgo[:, k] = part[:, k * B:(k + 1) * B].reshape(8, 16, B)
                else:
                    pgb[at(o), k] = part[:, k * B:(k + 1) * B]

    def sum_send(step, k, way):
        src = pgb.at[at(3 if way == 0 else -3), k] if step == 0 else pgs.at[way, k]
        return remote(
            src, pgr.at[way, step, k], pr_s.at[way, step, k], pr_r.at[way, step, k],
            up if way == 0 else down,
        )

    def far_send(k, way):
        return remote(
            pgb.at[at(4), k, pl.ds(way * 64, 64)], pgh.at[way, k], ph_s.at[way, k],
            ph_r.at[way, k], near(2 if way == 0 else -2, 0),
        )

    def sum_step(step, k, way):
        o = 3 - step if way == 0 else step - 3
        sum_send(step - 1, k, way).wait_recv()
        total = pgr[way, step - 1, k].astype(F32) + pgb[at(o), k].astype(F32)
        if step == 1:
            far_send(k, way).wait_recv()
            far = pgh[way, k].astype(F32)
            pgs[way, k, way * 64:way * 64 + 64] = (
                total[way * 64:way * 64 + 64] + far
            ).astype(BF16)
            pgs[way, k, 64 - way * 64:128 - way * 64] = total[
                64 - way * 64:128 - way * 64
            ].astype(BF16)
            go(sum_send(step, k, way))
        else:
            pga[way, :, k] = total.astype(BF16).reshape(8, 16, B)
        if step == 2 and k == 2:
            for r in range(8):
                go(remote(
                    pga.at[way, lax.rem(q + r, 8)], pgp.at[way + 1, q],
                    pa_s.at[way + 1, r], pa_r.at[way + 1, q], near(1 if way == 0 else -1, r),
                ))

    products(4)
    for k in range(3):
        for way in range(2):
            go(far_send(k, way))
    products(3, -3)
    for k in range(3):
        for way in range(2):
            go(sum_send(0, k, way))

    for c in p_copies:
        c.wait()
    for c in p_sends:
        c.wait_recv()
    for c in corr_sends:
        c.wait_recv()
    ig_sends = []
    for dy in (2, 1, 3, 0):
        pair = lax.rem(y + dy, 4)
        rows_of = corr[pl.ds(pl.multiple_of(pair * 256, 256), 256), :]
        for to in range(2):
            part = lax.dot_general(
                rows_of, pn[to], (((1,), (1,)), ((), ())), preferred_element_type=F32
            ).astype(BF16)
            for side in range(2):
                iga[2 * to + side, pair] = part[side * B:(side + 1) * B, 0:B]
                igb[pair, 2 * to + side] = part[side * B:(side + 1) * B, B:2 * B]
        if dy:
            ig_sends.append(remote(
                igb.at[pair], rb.at[dy], ip_s.at[1, dy], ip_r.at[1, dy], chip(0, dy)
            ))
            go(ig_sends[-1])
    for dx in (2, 1, 3):
        ig_sends.append(remote(
            iga.at[lax.rem(x + dx, 4)], ra.at[dx], ip_s.at[0, dx], ip_r.at[0, dx], chip(dx, 0)
        ))
        go(ig_sends[-1])

    products(2, -2)
    for k in range(3):
        for way in range(2):
            sum_step(1, k, way)
    products(1, -1, 0)
    pg_sends = []
    for r in range(1, 8):
        pg_sends.append(
            remote(
                pgo.at[lax.rem(q + r, 8)], pgp.at[0, q], pa_s.at[0, r], pa_r.at[0, r],
                plane(0, r),
            )
        )
        go(pg_sends[-1])
    pgp[0, q] = pgo[q]
    for k in range(3):
        for way in range(2):
            sum_step(2, k, way)

    for c in ig_sends:
        c.wait_recv()
    ig_last = []
    for d in (2, 1, 3):
        for mine, got, last, n in ((iga.at[x], ra, fa, 0), (igb.at[y], rb, fb, 1)):
            there = lax.rem((y if n == 0 else x) + d, 4)
            total = mine[there].astype(F32)
            for e in range(1, 4):
                total = total + got[e, there].astype(F32)
            out = igt.at[n, d]
            out[...] = total.astype(BF16)
            ig_last.append(remote(
                out, last.at[d], iq_s.at[n, d], iq_r.at[n, d],
                chip(0, d) if n == 0 else chip(d, 0),
            ))
            go(ig_last[-1])

    halves = []
    for mine, got, here in ((iga.at[x], ra, y), (igb.at[y], rb, x)):
        total = mine[here].astype(F32)
        for e in range(1, 4):
            total = total + got[e, here].astype(F32)
        halves.append(total)
    for c in ig_last:
        c.wait_recv()
    for n, last in ((0, fa), (1, fb)):
        total = halves[n]
        for e in range(1, 4):
            total = total + last[e].astype(F32)
        ig_ref[:, n * B:(n + 1) * B] = total.astype(BF16)

    for c in pg_sends:
        c.wait_recv()
    for s in range(8):
        for d in (1, 2):
            here = pgp.at[d, s]
            remote(here, here, pa_s.at[d, 0], pa_r.at[d, s], up).wait_recv()
        total = (
            pgp[0, s].astype(F32) + pgp[1, s].astype(F32) + pgp[2, s].astype(F32)
        ) * (8192.0 ** -0.5)
        pg_ref[:, :, s * B:(s + 1) * B] = total.astype(BF16)
    for c in sent:
        c.wait_send()


def per_device(inputs, cotangent, filters, projections):
    vmem = pl.BlockSpec(memory_space=pltpu.VMEM)
    dma = pltpu.SemaphoreType.DMA
    return pl.pallas_call(
        kernel,
        out_shape=(
            jax.ShapeDtypeStruct((B, 256), BF16),
            jax.ShapeDtypeStruct((3, 16, 1024), BF16),
        ),
        in_specs=[pl.BlockSpec(memory_space=pl.ANY)] * 4,
        out_specs=(vmem, vmem),
        scratch_shapes=[
            pltpu.VMEM((8, 8192 + B), F32),
            pltpu.VMEM((12, 8192), BF16),
            pltpu.VMEM((64, 1024), BF16),
            pltpu.VMEM((B, 1024), BF16),
            pltpu.VMEM((8, 384, 1024), BF16),
            pltpu.VMEM((8, 2, 8, 64, B), BF16),
            pltpu.VMEM((1, 1152, 256), BF16),
            pltpu.VMEM((4, 384, 256), F32),
            pltpu.VMEM((1024, 768), BF16),
            pltpu.VMEM((8, B, B), BF16),
            pltpu.VMEM((8, B, 1024), BF16),
            pltpu.VMEM((2, 256, 768), BF16),
            pltpu.VMEM((8, 3, B, B), BF16),
            pltpu.VMEM((2, 2, 3, B, B), BF16),
            pltpu.VMEM((2, 3, 64, B), BF16),
            pltpu.VMEM((2, 3, B, B), BF16),
            pltpu.VMEM((2, 8, 3, 16, B), BF16),
            pltpu.VMEM((8, 3, 16, B), BF16),
            pltpu.VMEM((3, 8, 3, 16, B), BF16),
            pltpu.VMEM((4, 4, B, B), BF16),
            pltpu.VMEM((4, 4, B, B), BF16),
            pltpu.VMEM((4, 4, B, B), BF16),
            pltpu.VMEM((4, 4, B, B), BF16),
            pltpu.VMEM((2, 4, B, B), BF16),
            pltpu.VMEM((4, B, B), BF16),
            pltpu.VMEM((4, B, B), BF16),
            dma((8,)), dma((8,)),
            dma((2, 4, 4)), dma((2, 4, 4)),
            dma((8,)), dma((8,)),
            dma((4,)), dma((4,)),
            dma((8,)), dma((8,)),
            dma, dma,
            dma((14,)),
            dma((2, 2, 3)), dma((2, 2, 3)),
            dma((2, 3)), dma((2, 3)),
            dma((3, 8)), dma((3, 8)),
            dma((6,)), dma((6,)),
            dma((4,)), dma((4,)),
            dma((2, 4)), dma((2, 4)),
            dma((2, 4)), dma((2, 4)),
        ],
        compiler_params=pltpu.CompilerParams(
            collective_id=0, has_side_effects=True, vmem_limit_bytes=48 * 1024 * 1024
        ),
        cost_estimate=pl.CostEstimate(
            flops=6_000_000_000, bytes_accessed=2_000_000, transcendentals=0
        ),
    )(*(
        pltpu.with_memory_space_constraint(a, pltpu.HBM)
        for a in (inputs, cotangent, filters, projections)
    ))


def solution(mesh):
    placed = (P("seq", None), P("seq", None), P(), P("filt", None, None))
    return jax.shard_map(
        per_device,
        mesh=mesh,
        in_specs=placed,
        out_specs=(P("seq", "filt"), P("filt", "seq", None)),
        check_vma=False,
    )
```

```python
import functools

import jax
import jax.numpy as jnp
from jax import lax
from jax.experimental import pallas as pl
from jax.experimental.pallas import tpu as pltpu
from jax.sharding import PartitionSpec as P

MESH = pl.DeviceIdType.MESH
F32 = jnp.float32
BF16 = jnp.bfloat16
B = 128
ORDER = (0, 1, -1, 2, -2, 3, -3, 4)


def kernel(
    x_ref, g_ref, f_ref, p_ref, ig_ref, pg_ref,
    taps, fv, gv, xv, hank, gl, g2, acc, corr, xs, xt, pn, pgb, pgr, pgh, pgs, pga, pgo, pgp,
    iga, igb, ra, rb, igt, fa, fb,
    ga_s, ga_r, gr_s, gr_r, gs_s, gs_r, ge_s, ge_r, xa_s, xa_r, xs_s, xs_r, loc,
    pr_s, pr_r, ph_s, ph_r, pa_s, pa_r, pp_s, pp_r, cs_s, cs_r, ip_s, ip_r, iq_s, iq_r,
):
    seq = lax.axis_index("seq")
    filt = lax.axis_index("filt")
    q, z = lax.div(seq, 8), lax.rem(seq, 8)
    xh, core = lax.div(filt, 2), lax.rem(filt, 2)
    x, y = xh * 2 + lax.rem(q, 2), lax.div(q, 2)
    sib = (seq, xh * 2 + 1 - core)
    up = (q * 8 + lax.rem(z + 1, 8), filt)
    down = (q * 8 + lax.rem(z + 7, 8), filt)

    def plane(dx, dq):
        return (lax.rem(q + dq, 8) * 8 + z, lax.rem(xh + dx, 2) * 2 + core)

    def remote(src, dst, send, recv, to):
        return pltpu.make_async_remote_copy(
            src_ref=src, dst_ref=dst, send_sem=send, recv_sem=recv,
            device_id=to, device_id_type=MESH,
        )

    sent = []

    def go(copy):
        copy.start()
        sent.append(copy)

    def settle(count):
        for c in sent[:count]:
            c.wait_send()
        del sent[:count]

    def chip(dx, dy):
        to_x, to_y = lax.rem(x + dx, 4), lax.rem(y + dy, 4)
        return ((to_y * 2 + lax.rem(to_x, 2)) * 8 + z, lax.div(to_x, 2) * 2 + core)

    def near(dz, dq):
        return (lax.rem(q + dq, 8) * 8 + lax.rem(z + dz + 8, 8), filt)

    barrier = pltpu.get_barrier_semaphore()
    partners = (
        [plane(0, r) for r in range(1, 8)]
        + [((y * 2 + side) * 8 + z, (1 - xh) * 2 + core) for side in range(2)]
        + [up, down, sib]
    )
    for to in partners:
        pl.semaphore_signal(barrier, inc=1, device_id=to, device_id_type=MESH)

    rows = pl.ds(pl.multiple_of(core * 64, 64), 64)
    lanes = pl.ds(pl.multiple_of(q * B, B), B)
    own = pl.ds(pl.multiple_of(core * 384, 128), 384)

    def p_slice(k, to, of_core):
        e = pl.ds(pl.multiple_of(to * 512 + of_core * 256, 256), 256)
        return p_ref.at[k, e, lanes]

    def p_place(k, to):
        return pn.at[to, :, pl.ds(pl.multiple_of(core * 384 + k * B, B), B)]

    f_in = pltpu.make_async_copy(f_ref, fv, loc.at[4])
    g_own = pltpu.make_async_copy(g_ref.at[rows, lanes], gl.at[0, core, q], loc.at[6])
    g_in = pltpu.make_async_copy(g_ref.at[rows], gv, loc.at[5])
    x_in = pltpu.make_async_copy(x_ref, xv, loc.at[7])
    p_copies = [
        pltpu.make_async_copy(p_slice(k, to, core), p_place(k, to), loc.at[8 + 2 * k + to])
        for k in range(3)
        for to in range(2)
    ]
    for c in [g_in, g_own, f_in, x_in] + p_copies:
        c.start()
    f_in.wait()
    pick = jnp.where(
        lax.broadcasted_iota(jnp.int32, (8, 12), 1)
        == lax.broadcasted_iota(jnp.int32, (8, 12), 0) + 3 * filt,
        1.0, 0.0,
    ).astype(BF16)
    taps[:, 0:B] = jnp.zeros((8, B), F32)
    taps[:, B:] = jnp.dot(pick, fv[...], preferred_element_type=F32)
    g2[0, 1024:1152, 0:B] = jnp.zeros((B, B), BF16)
    g2[0, 896:1152, B:2 * B] = jnp.zeros((2 * B, B), BF16)

    def build(j, carry):
        for i in range(8):
            upper = lax.broadcasted_iota(jnp.int32, (16, B), 1) >= (
                lax.broadcasted_iota(jnp.int32, (16, B), 0) + 16 * i
            )
            for k in range(3):
                before = None
                for d in range(-1, 8):
                    row = taps[k:k + 1, pl.ds(pl.multiple_of((8 * j + d + 1) * B, B), B)]
                    turned = pltpu.roll(
                        jnp.broadcast_to(row, (16, B)), 16 * i, 1, stride=1, stride_axis=0
                    )
                    if d >= 0:
                        hank[d, k * B + 16 * i:k * B + 16 * i + 16,
                             pl.ds(pl.multiple_of(j * B, B), B)] = jnp.where(
                                 upper, turned, before
                             ).astype(BF16)
                    before = turned
        return carry

    lax.fori_loop(0, 4, build, 0)
    g_in.wait()
    g_own.wait()

    pl.semaphore_wait(barrier, len(partners))

    for n, (dy, side) in enumerate(((2, 1), (2, 0), (1, 1), (3, 1), (1, 0), (3, 0), (0, 1))):
        to_q = lax.rem(y + dy, 4) * 2 + lax.rem(x + side, 2)
        col = pl.ds(pl.multiple_of(to_q * B, B), B)
        go(remote(
            gv.at[:, col], gl.at[0, core, q], ga_s.at[n], ga_r.at[q], (to_q * 8 + z, filt)
        ))
    p_sends = [
        remote(
            p_slice(k, to, 1 - core), p_place(k, to), pp_s.at[2 * k + to], pp_r.at[2 * k + to], sib
        )
        for k in range(3)
        for to in range(2)
    ]
    for c in p_sends:
        go(c)
    lax.fori_loop(4, 8, build, 0)

    x_in.wait()
    for t in range(8):
        flip = xv[:, t * B:(t + 1) * B].T
        for zz in range(8):
            xs[zz, t * 16:(t + 1) * 16, :] = flip[zz * 16:(zz + 1) * 16]
    half = pl.ds(core * 4, 4)
    x_own = pltpu.make_async_copy(xs.at[half], xt.at[half, :, lanes], loc.at[3])
    x_own.start()

    def turn(s):
        return lax.rem(y + (0, 1, 3, 2)[s], 4)

    def sub(slot, s):
        return gl.at[slot, core, pl.ds(turn(s) * 2, 2)]

    def ring_send(step, s, way):
        here = -step % 8 if way == 0 else step
        there = (-step - 1) % 8 if way == 0 else step + 1
        return remote(
            sub(here, s), sub(there, s),
            gr_s.at[way, step, s], gr_r.at[way, step, s], up if way == 0 else down,
        )

    def hand_over(slot):
        mine = gl.at[slot, core]
        return remote(mine, mine, gs_s.at[slot], gs_r.at[slot], sib)

    def handed(slot):
        other = gl.at[slot, 1 - core]
        return remote(other, other, gs_s.at[slot], gs_r.at[slot], sib)

    def landed(from_q):
        here = gl.at[0, core, from_q]
        remote(here, here, ga_s.at[0], ga_r.at[from_q], up).wait_recv()

    landed(lax.div(q, 2) * 2 + lax.rem(q + 1, 2))
    for s in range(4):
        if s:
            landed(turn(s) * 2)
            landed(turn(s) * 2 + 1)
        for way in range(2):
            go(ring_send(0, s, way))
    go(hand_over(0))

    x_sends = []
    for r in range(1, 8):
        x_sends.append(
            remote(xs.at[half], xt.at[half, :, lanes], xa_s.at[r], xa_r.at[r], plane(0, r))
        )
        go(x_sends[-1])

    corr_sends = []

    def conv(o):
        slot = o % 8
        if o == 4:
            for s in range(4):
                other = gl.at[4, 1 - core, pl.ds(turn(s) * 2, 2)]
                remote(other, other, ge_s.at[s], ge_r.at[s], sib).wait_recv()
        else:
            handed(slot).wait_recv()
        buf = g2.at[0]
        for m in range(8):
            for h in range(2):
                piece = gl[slot, h, m]
                buf[m * B + h * 64:m * B + h * 64 + 64, 0:B] = piece
                if m > 0:
                    buf[(m - 1) * B + h * 64:(m - 1) * B + h * 64 + 64, B:2 * B] = piece
        wrap = jnp.where(lax.rem(z + o + 8, 8) < z, 1, 0)
        for p in range(4):
            depth = B * (8 - 2 * p)
            start = pl.multiple_of(wrap * B + 2 * p * B, B)
            term = jnp.dot(
                hank[slot, :, 0:depth], buf[pl.ds(start, depth), :],
                preferred_element_type=F32,
            )
            if o == 0:
                acc[p] = term
            elif o != 4:
                acc[p] += term
            else:
                done = (acc[p] + term).astype(BF16)
                for e in range(2):
                    for k in range(3):
                        corr[
                            (2 * p + e) * B:(2 * p + e + 1) * B,
                            pl.ds(pl.multiple_of(core * 384 + k * B, B), B),
                        ] = done[k * B:(k + 1) * B, e * B:(e + 1) * B]
                mine = corr.at[pl.ds(p * 256, 256), own]
                corr_sends.append(remote(mine, mine, cs_s.at[p], cs_r.at[p], sib))
                go(corr_sends[-1])

    conv(0)
    for step in range(1, 4):
        for s in range(4):
            for way in range(2):
                ring_send(step - 1, s, way).wait_recv()
                if step < 3 or s // 2 == way:
                    go(ring_send(step, s, way))
        go(hand_over(-step % 8))
        go(hand_over(step))
        if step > 1:
            conv(step - 1)
            conv(1 - step)
        if step == 3:
            x_own.wait()
            for c in x_sends:
                c.wait_recv()
            x_hand = remote(xt.at[half], xt.at[half], xs_s, xs_r, sib)
            go(x_hand)
    early = len(sent)
    conv(3)
    for s in range(4):
        ring_send(3, s, s // 2).wait_recv()
        mine = sub(4, s)
        go(remote(mine, mine, ge_s.at[s], ge_r.at[s], sib))
    conv(-3)
    conv(4)

    half_o = pl.ds((1 - core) * 4, 4)
    remote(xt.at[half_o], xt.at[half_o], xs_s, xs_r, sib).wait_recv()

    def at(o):
        return lax.rem(z + o + 8, 8)

    def products(*offsets):
        for o in offsets:
            part = jnp.dot(xt[at(o)], corr[:, own], preferred_element_type=F32).astype(BF16)
            for k in range(3):
                if o == 0:
                    pgo[:, k] = part[:, k * B:(k + 1) * B].reshape(8, 16, B)
                else:
                    pgb[at(o), k] = part[:, k * B:(k + 1) * B]

    def sum_send(step, k, way):
        src = pgb.at[at(3 if way == 0 else -3), k] if step == 0 else pgs.at[way, k]
        return remote(
            src, pgr.at[way, step, k], pr_s.at[way, step, k], pr_r.at[way, step, k],
            up if way == 0 else down,
        )

    def far_send(k, way):
        return remote(
            pgb.at[at(4), k, pl.ds(way * 64, 64)], pgh.at[way, k], ph_s.at[way, k],
            ph_r.at[way, k], near(2 if way == 0 else -2, 0),
        )

    def sum_step(step, k, way):
        o = 3 - step if way == 0 else step - 3
        sum_send(step - 1, k, way).wait_recv()
        total = pgr[way, step - 1, k].astype(F32) + pgb[at(o), k].astype(F32)
        if step == 1:
            far_send(k, way).wait_recv()
            far = pgh[way, k].astype(F32)
            pgs[way, k, way * 64:way * 64 + 64] = (
                total[way * 64:way * 64 + 64] + far
            ).astype(BF16)
            pgs[way, k, 64 - way * 64:128 - way * 64] = total[
                64 - way * 64:128 - way * 64
            ].astype(BF16)
            go(sum_send(step, k, way))
        else:
            pga[way, :, k] = total.astype(BF16).reshape(8, 16, B)
        if step == 2 and k == 2:
            for r in range(8):
                go(remote(
                    pga.at[way, lax.rem(q + r, 8)], pgp.at[way + 1, q],
                    pa_s.at[way + 1, r], pa_r.at[way + 1, q], near(1 if way == 0 else -1, r),
                ))

    products(4)
    for k in range(3):
        for way in range(2):
            go(far_send(k, way))
    products(3, -3)
    for k in range(3):
        for way in range(2):
            go(sum_send(0, k, way))

    for c in p_copies:
        c.wait()
    for c in p_sends:
        c.wait_recv()
    for c in corr_sends:
        c.wait_recv()
    ig_sends = []
    for dy in (2, 1, 3, 0):
        pair = lax.rem(y + dy, 4)
        rows_of = corr[pl.ds(pl.multiple_of(pair * 256, 256), 256), :]
        for to in range(2):
            part = lax.dot_general(
                rows_of, pn[to], (((1,), (1,)), ((), ())), preferred_element_type=F32
            ).astype(BF16)
            for side in range(2):
                iga[2 * to + side, pair] = part[side * B:(side + 1) * B, 0:B]
                igb[pair, 2 * to + side] = part[side * B:(side + 1) * B, B:2 * B]
        if dy:
            ig_sends.append(remote(
                igb.at[pair], rb.at[dy], ip_s.at[1, dy], ip_r.at[1, dy], chip(0, dy)
            ))
            go(ig_sends[-1])
    for dx in (2, 1, 3):
        ig_sends.append(remote(
            iga.at[lax.rem(x + dx, 4)], ra.at[dx], ip_s.at[0, dx], ip_r.at[0, dx], chip(dx, 0)
        ))
        go(ig_sends[-1])

    products(2, -2)
    settle(early)
    for k in range(3):
        for way in range(2):
            sum_step(1, k, way)
    products(1, -1, 0)
    pg_sends = []
    for r in range(1, 8):
        pg_sends.append(
            remote(
                pgo.at[lax.rem(q + r, 8)], pgp.at[0, q], pa_s.at[0, r], pa_r.at[0, r],
                plane(0, r),
            )
        )
        go(pg_sends[-1])
    pgp[0, q] = pgo[q]
    for k in range(3):
        for way in range(2):
            sum_step(2, k, way)

    middle = len(sent) - 23
    for c in ig_sends:
        c.wait_recv()
    ig_last = []
    for d in (2, 1, 3):
        for mine, got, last, n in ((iga.at[x], ra, fa, 0), (igb.at[y], rb, fb, 1)):
            there = lax.rem((y if n == 0 else x) + d, 4)
            total = mine[there].astype(F32)
            for e in range(1, 4):
                total = total + got[e, there].astype(F32)
            out = igt.at[n, d]
            out[...] = total.astype(BF16)
            ig_last.append(remote(
                out, last.at[d], iq_s.at[n, d], iq_r.at[n, d],
                chip(0, d) if n == 0 else chip(d, 0),
            ))
            go(ig_last[-1])

    settle(middle)
    halves = []
    for mine, got, here in ((iga.at[x], ra, y), (igb.at[y], rb, x)):
        total = mine[here].astype(F32)
        for e in range(1, 4):
            total = total + got[e, here].astype(F32)
        halves.append(total)
    for c in ig_last:
        c.wait_recv()
    for n, last in ((0, fa), (1, fb)):
        total = halves[n]
        for e in range(1, 4):
            total = total + last[e].astype(F32)
        ig_ref[:, n * B:(n + 1) * B] = total.astype(BF16)

    for c in pg_sends:
        c.wait_recv()
    for s in range(8):
        for d in (1, 2):
            here = pgp.at[d, s]
            remote(here, here, pa_s.at[d, 0], pa_r.at[d, s], up).wait_recv()
        total = (
            pgp[0, s].astype(F32) + pgp[1, s].astype(F32) + pgp[2, s].astype(F32)
        ) * (8192.0 ** -0.5)
        pg_ref[:, :, s * B:(s + 1) * B] = total.astype(BF16)
    settle(len(sent))


def per_device(inputs, cotangent, filters, projections):
    vmem = pl.BlockSpec(memory_space=pltpu.VMEM)
    dma = pltpu.SemaphoreType.DMA
    return pl.pallas_call(
        kernel,
        out_shape=(
            jax.ShapeDtypeStruct((B, 256), BF16),
            jax.ShapeDtypeStruct((3, 16, 1024), BF16),
        ),
        in_specs=[pl.BlockSpec(memory_space=pl.ANY)] * 4,
        out_specs=(vmem, vmem),
        scratch_shapes=[
            pltpu.VMEM((8, 8192 + B), F32),
            pltpu.VMEM((12, 8192), BF16),
            pltpu.VMEM((64, 1024), BF16),
            pltpu.VMEM((B, 1024), BF16),
            pltpu.VMEM((8, 384, 1024), BF16),
            pltpu.VMEM((8, 2, 8, 64, B), BF16),
            pltpu.VMEM((1, 1152, 256), BF16),
            pltpu.VMEM((4, 384, 256), F32),
            pltpu.VMEM((1024, 768), BF16),
            pltpu.VMEM((8, B, B), BF16),
            pltpu.VMEM((8, B, 1024), BF16),
            pltpu.VMEM((2, 256, 768), BF16),
            pltpu.VMEM((8, 3, B, B), BF16),
            pltpu.VMEM((2, 2, 3, B, B), BF16),
            pltpu.VMEM((2, 3, 64, B), BF16),
            pltpu.VMEM((2, 3, B, B), BF16),
            pltpu.VMEM((2, 8, 3, 16, B), BF16),
            pltpu.VMEM((8, 3, 16, B), BF16),
            pltpu.VMEM((3, 8, 3, 16, B), BF16),
            pltpu.VMEM((4, 4, B, B), BF16),
            pltpu.VMEM((4, 4, B, B), BF16),
            pltpu.VMEM((4, 4, B, B), BF16),
            pltpu.VMEM((4, 4, B, B), BF16),
            pltpu.VMEM((2, 4, B, B), BF16),
            pltpu.VMEM((4, B, B), BF16),
            pltpu.VMEM((4, B, B), BF16),
            dma((8,)), dma((8,)),
            dma((2, 4, 4)), dma((2, 4, 4)),
            dma((8,)), dma((8,)),
            dma((4,)), dma((4,)),
            dma((8,)), dma((8,)),
            dma, dma,
            dma((14,)),
            dma((2, 2, 3)), dma((2, 2, 3)),
            dma((2, 3)), dma((2, 3)),
            dma((3, 8)), dma((3, 8)),
            dma((6,)), dma((6,)),
            dma((4,)), dma((4,)),
            dma((2, 4)), dma((2, 4)),
            dma((2, 4)), dma((2, 4)),
        ],
        compiler_params=pltpu.CompilerParams(
            collective_id=0, has_side_effects=True, vmem_limit_bytes=48 * 1024 * 1024
        ),
        cost_estimate=pl.CostEstimate(
            flops=6_000_000_000, bytes_accessed=2_000_000, transcendentals=0
        ),
    )(*(
        pltpu.with_memory_space_constraint(a, pltpu.HBM)
        for a in (inputs, cotangent, filters, projections)
    ))


def solution(mesh):
    placed = (P("seq", None), P("seq", None), P(), P("filt", None, None))
    return jax.shard_map(
        per_device,
        mesh=mesh,
        in_specs=placed,
        out_specs=(P("seq", "filt"), P("filt", "seq", None)),
        check_vma=False,
    )
```

```python
import functools

import jax
import jax.numpy as jnp
from jax import lax
from jax.experimental import pallas as pl
from jax.experimental.pallas import tpu as pltpu
from jax.sharding import PartitionSpec as P

MESH = pl.DeviceIdType.MESH
F32 = jnp.float32
BF16 = jnp.bfloat16
B = 128
ORDER = (0, 1, -1, 2, -2, 3, -3, 4)


def kernel(
    x_ref, g_ref, f_ref, p_ref, ig_ref, pg_ref,
    taps, fv, gv, xv, hank, gl, g2, acc, corr, xs, xt, pn, pgb, pgr, pgh, pgs, pga, pgo, pgp,
    iga, igb, ra, rb, igt, fa, fb,
    ga_s, ga_r, gr_s, gr_r, gs_s, gs_r, ge_s, ge_r, xa_s, xa_r, xs_s, xs_r, loc,
    pr_s, pr_r, ph_s, ph_r, pa_s, pa_r, pp_s, pp_r, cs_s, cs_r, ip_s, ip_r, iq_s, iq_r,
):
    seq = lax.axis_index("seq")
    filt = lax.axis_index("filt")
    q, z = lax.div(seq, 8), lax.rem(seq, 8)
    xh, core = lax.div(filt, 2), lax.rem(filt, 2)
    x, y = xh * 2 + lax.rem(q, 2), lax.div(q, 2)
    sib = (seq, xh * 2 + 1 - core)
    up = (q * 8 + lax.rem(z + 1, 8), filt)
    down = (q * 8 + lax.rem(z + 7, 8), filt)

    def plane(dx, dq):
        return (lax.rem(q + dq, 8) * 8 + z, lax.rem(xh + dx, 2) * 2 + core)

    def remote(src, dst, send, recv, to):
        return pltpu.make_async_remote_copy(
            src_ref=src, dst_ref=dst, send_sem=send, recv_sem=recv,
            device_id=to, device_id_type=MESH,
        )

    sent = []

    def go(copy):
        copy.start()
        sent.append(copy)

    def settle(count):
        for c in sent[:count]:
            c.wait_send()
        del sent[:count]

    def chip(dx, dy):
        to_x, to_y = lax.rem(x + dx, 4), lax.rem(y + dy, 4)
        return ((to_y * 2 + lax.rem(to_x, 2)) * 8 + z, lax.div(to_x, 2) * 2 + core)

    def near(dz, dq):
        return (lax.rem(q + dq, 8) * 8 + lax.rem(z + dz + 8, 8), filt)

    barrier = pltpu.get_barrier_semaphore()
    partners = (
        [plane(0, r) for r in range(1, 8)]
        + [((y * 2 + side) * 8 + z, (1 - xh) * 2 + core) for side in range(2)]
        + [up, down, sib]
    )
    for to in partners:
        pl.semaphore_signal(barrier, inc=1, device_id=to, device_id_type=MESH)

    rows = pl.ds(pl.multiple_of(core * 64, 64), 64)
    lanes = pl.ds(pl.multiple_of(q * B, B), B)
    own = pl.ds(pl.multiple_of(core * 384, 128), 384)

    def p_slice(k, to, of_core):
        e = pl.ds(pl.multiple_of(to * 512 + of_core * 256, 256), 256)
        return p_ref.at[k, e, lanes]

    def p_place(k, to):
        return pn.at[to, :, pl.ds(pl.multiple_of(core * 384 + k * B, B), B)]

    f_in = pltpu.make_async_copy(f_ref, fv, loc.at[4])
    g_own = pltpu.make_async_copy(g_ref.at[rows, lanes], gl.at[0, core, q], loc.at[6])
    g_in = pltpu.make_async_copy(g_ref.at[rows], gv, loc.at[5])
    x_in = pltpu.make_async_copy(x_ref, xv, loc.at[7])
    p_copies = [
        pltpu.make_async_copy(p_slice(k, to, core), p_place(k, to), loc.at[8 + 2 * k + to])
        for k in range(3)
        for to in range(2)
    ]
    for c in [g_in, g_own, f_in, x_in] + p_copies:
        c.start()
    f_in.wait()
    pick = jnp.where(
        lax.broadcasted_iota(jnp.int32, (8, 12), 1)
        == lax.broadcasted_iota(jnp.int32, (8, 12), 0) + 3 * filt,
        1.0, 0.0,
    ).astype(BF16)
    taps[:, 0:B] = jnp.zeros((8, B), F32)
    taps[:, B:] = jnp.dot(pick, fv[...], preferred_element_type=F32)
    g2[0, 1024:1152, 0:B] = jnp.zeros((B, B), BF16)
    g2[0, 896:1152, B:2 * B] = jnp.zeros((2 * B, B), BF16)

    def build(j, carry):
        for i in range(8):
            upper = lax.broadcasted_iota(jnp.int32, (16, B), 1) >= (
                lax.broadcasted_iota(jnp.int32, (16, B), 0) + 16 * i
            )
            for k in range(3):
                before = None
                for d in range(-1, 8):
                    row = taps[k:k + 1, pl.ds(pl.multiple_of((8 * j + d + 1) * B, B), B)]
                    turned = pltpu.roll(
                        jnp.broadcast_to(row, (16, B)), 16 * i, 1, stride=1, stride_axis=0
                    )
                    if d >= 0:
                        hank[d, k * B + 16 * i:k * B + 16 * i + 16,
                             pl.ds(pl.multiple_of(j * B, B), B)] = jnp.where(
                                 upper, turned, before
                             ).astype(BF16)
                    before = turned
        return carry

    lax.fori_loop(0, 4, build, 0)
    g_in.wait()
    g_own.wait()

    pl.semaphore_wait(barrier, len(partners))

    for n, (dy, side) in enumerate(((2, 1), (2, 0), (1, 1), (3, 1), (1, 0), (3, 0), (0, 1))):
        to_q = lax.rem(y + dy, 4) * 2 + lax.rem(x + side, 2)
        col = pl.ds(pl.multiple_of(to_q * B, B), B)
        go(remote(
            gv.at[:, col], gl.at[0, core, q], ga_s.at[n], ga_r.at[q], (to_q * 8 + z, filt)
        ))
    p_sends = [
        remote(
            p_slice(k, to, 1 - core), p_place(k, to), pp_s.at[2 * k + to], pp_r.at[2 * k + to], sib
        )
        for k in range(3)
        for to in range(2)
    ]
    for c in p_sends:
        go(c)
    lax.fori_loop(4, 8, build, 0)

    x_in.wait()
    for t in range(8):
        flip = xv[:, t * B:(t + 1) * B].T
        for zz in range(8):
            xs[zz, t * 16:(t + 1) * 16, :] = flip[zz * 16:(zz + 1) * 16]
    half = pl.ds(core * 4, 4)
    x_own = pltpu.make_async_copy(xs.at[half], xt.at[half, :, lanes], loc.at[3])
    x_own.start()

    def turn(s):
        return lax.rem(y + (0, 1, 3, 2)[s], 4)

    def sub(slot, s):
        return gl.at[slot, core, pl.ds(turn(s) * 2, 2)]

    def ring_send(step, s, way):
        here = -step % 8 if way == 0 else step
        there = (-step - 1) % 8 if way == 0 else step + 1
        return remote(
            sub(here, s), sub(there, s),
            gr_s.at[way, step, s], gr_r.at[way, step, s], up if way == 0 else down,
        )

    def hand_over(slot):
        mine = gl.at[slot, core]
        return remote(mine, mine, gs_s.at[slot], gs_r.at[slot], sib)

    def handed(slot):
        other = gl.at[slot, 1 - core]
        return remote(other, other, gs_s.at[slot], gs_r.at[slot], sib)

    def landed(from_q):
        here = gl.at[0, core, from_q]
        remote(here, here, ga_s.at[0], ga_r.at[from_q], up).wait_recv()

    landed(lax.div(q, 2) * 2 + lax.rem(q + 1, 2))
    for s in range(4):
        if s:
            landed(turn(s) * 2)
            landed(turn(s) * 2 + 1)
        for way in range(2):
            go(ring_send(0, s, way))
    go(hand_over(0))

    x_sends = []
    for r in range(1, 8):
        x_sends.append(
            remote(xs.at[half], xt.at[half, :, lanes], xa_s.at[r], xa_r.at[r], plane(0, r))
        )
        go(x_sends[-1])

    corr_sends = []

    def conv(o):
        slot = o % 8
        if o == 4:
            for s in range(4):
                other = gl.at[4, 1 - core, pl.ds(turn(s) * 2, 2)]
                remote(other, other, ge_s.at[s], ge_r.at[s], sib).wait_recv()
        else:
            handed(slot).wait_recv()
        buf = g2.at[0]
        for m in range(8):
            for h in range(2):
                piece = gl[slot, h, m]
                buf[m * B + h * 64:m * B + h * 64 + 64, 0:B] = piece
                if m > 0:
                    buf[(m - 1) * B + h * 64:(m - 1) * B + h * 64 + 64, B:2 * B] = piece
        wrap = jnp.where(lax.rem(z + o + 8, 8) < z, 1, 0)
        for p in range(4):
            depth = B * (8 - 2 * p)
            start = pl.multiple_of(wrap * B + 2 * p * B, B)
            term = jnp.dot(
                hank[slot, :, 0:depth], buf[pl.ds(start, depth), :],
                preferred_element_type=F32,
            )
            if o == 0:
                acc[p] = term
            elif o != 4:
                acc[p] += term
            else:
                done = (acc[p] + term).astype(BF16)
                for e in range(2):
                    for k in range(3):
                        corr[
                            (2 * p + e) * B:(2 * p + e + 1) * B,
                            pl.ds(pl.multiple_of(core * 384 + k * B, B), B),
                        ] = done[k * B:(k + 1) * B, e * B:(e + 1) * B]
                mine = corr.at[pl.ds(p * 256, 256), own]
                corr_sends.append(remote(mine, mine, cs_s.at[p], cs_r.at[p], sib))
                go(corr_sends[-1])

    conv(0)
    for step in range(1, 4):
        for s in range(4):
            for way in range(2):
                ring_send(step - 1, s, way).wait_recv()
                if step < 3 or s // 2 == way:
                    go(ring_send(step, s, way))
        go(hand_over(-step % 8))
        go(hand_over(step))
        if step > 1:
            conv(step - 1)
            conv(1 - step)
        if step == 3:
            x_own.wait()
            for c in x_sends:
                c.wait_recv()
            x_hand = remote(xt.at[half], xt.at[half], xs_s, xs_r, sib)
            go(x_hand)
    early = len(sent)
    conv(3)
    for s in range(4):
        ring_send(3, s, s // 2).wait_recv()
        mine = sub(4, s)
        go(remote(mine, mine, ge_s.at[s], ge_r.at[s], sib))
    conv(-3)
    conv(4)

    half_o = pl.ds((1 - core) * 4, 4)
    remote(xt.at[half_o], xt.at[half_o], xs_s, xs_r, sib).wait_recv()

    def at(o):
        return lax.rem(z + o + 8, 8)

    def products(*offsets):
        for o in offsets:
            part = jnp.dot(xt[at(o)], corr[:, own], preferred_element_type=F32).astype(BF16)
            for k in range(3):
                if o == 0:
                    pgo[:, k] = part[:, k * B:(k + 1) * B].reshape(8, 16, B)
                else:
                    pgb[at(o), k] = part[:, k * B:(k + 1) * B]

    def sum_send(step, k, way):
        src = pgb.at[at(3 if way == 0 else -3), k] if step == 0 else pgs.at[way, k]
        return remote(
            src, pgr.at[way, step, k], pr_s.at[way, step, k], pr_r.at[way, step, k],
            up if way == 0 else down,
        )

    def far_send(k, way):
        return remote(
            pgb.at[at(4), k, pl.ds(way * 64, 64)], pgh.at[way, k], ph_s.at[way, k],
            ph_r.at[way, k], near(2 if way == 0 else -2, 0),
        )

    def sum_step(step, k, way):
        o = 3 - step if way == 0 else step - 3
        sum_send(step - 1, k, way).wait_recv()
        total = pgr[way, step - 1, k].astype(F32) + pgb[at(o), k].astype(F32)
        if step == 1:
            far_send(k, way).wait_recv()
            far = pgh[way, k].astype(F32)
            pgs[way, k, way * 64:way * 64 + 64] = (
                total[way * 64:way * 64 + 64] + far
            ).astype(BF16)
            pgs[way, k, 64 - way * 64:128 - way * 64] = total[
                64 - way * 64:128 - way * 64
            ].astype(BF16)
            go(sum_send(step, k, way))
        else:
            pga[way, :, k] = total.astype(BF16).reshape(8, 16, B)
        if step == 2 and k == 2:
            for r in range(8):
                go(remote(
                    pga.at[way, lax.rem(q + r, 8)], pgp.at[way + 1, q],
                    pa_s.at[way + 1, r], pa_r.at[way + 1, q], near(1 if way == 0 else -1, r),
                ))

    products(4, 3, -3)
    for k in range(3):
        for way in range(2):
            go(far_send(k, way))
            go(sum_send(0, k, way))

    for c in p_copies:
        c.wait()
    for c in p_sends:
        c.wait_recv()
    for c in corr_sends:
        c.wait_recv()
    ig_sends = []
    for dy in (2, 1, 3, 0):
        pair = lax.rem(y + dy, 4)
        rows_of = corr[pl.ds(pl.multiple_of(pair * 256, 256), 256), :]
        for to in range(2):
            part = lax.dot_general(
                rows_of, pn[to], (((1,), (1,)), ((), ())), preferred_element_type=F32
            ).astype(BF16)
            for side in range(2):
                iga[2 * to + side, pair] = part[side * B:(side + 1) * B, 0:B]
                igb[pair, 2 * to + side] = part[side * B:(side + 1) * B, B:2 * B]
        if dy:
            ig_sends.append(remote(
                igb.at[pair], rb.at[dy], ip_s.at[1, dy], ip_r.at[1, dy], chip(0, dy)
            ))
            go(ig_sends[-1])
    for dx in (2, 1, 3):
        ig_sends.append(remote(
            iga.at[lax.rem(x + dx, 4)], ra.at[dx], ip_s.at[0, dx], ip_r.at[0, dx], chip(dx, 0)
        ))
        go(ig_sends[-1])

    products(2, -2)
    settle(early)
    for k in range(3):
        for way in range(2):
            sum_step(1, k, way)
    products(1, -1, 0)
    pg_sends = []
    for r in range(1, 8):
        pg_sends.append(
            remote(
                pgo.at[lax.rem(q + r, 8)], pgp.at[0, q], pa_s.at[0, r], pa_r.at[0, r],
                plane(0, r),
            )
        )
        go(pg_sends[-1])
    pgp[0, q] = pgo[q]
    for k in range(3):
        for way in range(2):
            sum_step(2, k, way)

    middle = len(sent) - 23
    for c in ig_sends:
        c.wait_recv()
    ig_last = []
    for d in (2, 1, 3):
        for mine, got, last, n in ((iga.at[x], ra, fa, 0), (igb.at[y], rb, fb, 1)):
            there = lax.rem((y if n == 0 else x) + d, 4)
            total = mine[there].astype(F32)
            for e in range(1, 4):
                total = total + got[e, there].astype(F32)
            out = igt.at[n, d]
            out[...] = total.astype(BF16)
            ig_last.append(remote(
                out, last.at[d], iq_s.at[n, d], iq_r.at[n, d],
                chip(0, d) if n == 0 else chip(d, 0),
            ))
            go(ig_last[-1])

    settle(middle)
    halves = []
    for mine, got, here in ((iga.at[x], ra, y), (igb.at[y], rb, x)):
        total = mine[here].astype(F32)
        for e in range(1, 4):
            total = total + got[e, here].astype(F32)
        halves.append(total)
    for c in ig_last:
        c.wait_recv()
    for n, last in ((0, fa), (1, fb)):
        total = halves[n]
        for e in range(1, 4):
            total = total + last[e].astype(F32)
        ig_ref[:, n * B:(n + 1) * B] = total.astype(BF16)

    for c in pg_sends:
        c.wait_recv()
    for s in range(8):
        for d in (1, 2):
            here = pgp.at[d, s]
            remote(here, here, pa_s.at[d, 0], pa_r.at[d, s], up).wait_recv()
        total = (
            pgp[0, s].astype(F32) + pgp[1, s].astype(F32) + pgp[2, s].astype(F32)
        ) * (8192.0 ** -0.5)
        pg_ref[:, :, s * B:(s + 1) * B] = total.astype(BF16)
    settle(len(sent))


def per_device(inputs, cotangent, filters, projections):
    vmem = pl.BlockSpec(memory_space=pltpu.VMEM)
    dma = pltpu.SemaphoreType.DMA
    return pl.pallas_call(
        kernel,
        out_shape=(
            jax.ShapeDtypeStruct((B, 256), BF16),
            jax.ShapeDtypeStruct((3, 16, 1024), BF16),
        ),
        in_specs=[pl.BlockSpec(memory_space=pl.ANY)] * 4,
        out_specs=(vmem, vmem),
        scratch_shapes=[
            pltpu.VMEM((8, 8192 + B), F32),
            pltpu.VMEM((12, 8192), BF16),
            pltpu.VMEM((64, 1024), BF16),
            pltpu.VMEM((B, 1024), BF16),
            pltpu.VMEM((8, 384, 1024), BF16),
            pltpu.VMEM((8, 2, 8, 64, B), BF16),
            pltpu.VMEM((1, 1152, 256), BF16),
            pltpu.VMEM((4, 384, 256), F32),
            pltpu.VMEM((1024, 768), BF16),
            pltpu.VMEM((8, B, B), BF16),
            pltpu.VMEM((8, B, 1024), BF16),
            pltpu.VMEM((2, 256, 768), BF16),
            pltpu.VMEM((8, 3, B, B), BF16),
            pltpu.VMEM((2, 2, 3, B, B), BF16),
            pltpu.VMEM((2, 3, 64, B), BF16),
            pltpu.VMEM((2, 3, B, B), BF16),
            pltpu.VMEM((2, 8, 3, 16, B), BF16),
            pltpu.VMEM((8, 3, 16, B), BF16),
            pltpu.VMEM((3, 8, 3, 16, B), BF16),
            pltpu.VMEM((4, 4, B, B), BF16),
            pltpu.VMEM((4, 4, B, B), BF16),
            pltpu.VMEM((4, 4, B, B), BF16),
            pltpu.VMEM((4, 4, B, B), BF16),
            pltpu.VMEM((2, 4, B, B), BF16),
            pltpu.VMEM((4, B, B), BF16),
            pltpu.VMEM((4, B, B), BF16),
            dma((8,)), dma((8,)),
            dma((2, 4, 4)), dma((2, 4, 4)),
            dma((8,)), dma((8,)),
            dma((4,)), dma((4,)),
            dma((8,)), dma((8,)),
            dma, dma,
            dma((14,)),
            dma((2, 2, 3)), dma((2, 2, 3)),
            dma((2, 3)), dma((2, 3)),
            dma((3, 8)), dma((3, 8)),
            dma((6,)), dma((6,)),
            dma((4,)), dma((4,)),
            dma((2, 4)), dma((2, 4)),
            dma((2, 4)), dma((2, 4)),
        ],
        compiler_params=pltpu.CompilerParams(
            collective_id=0, has_side_effects=True, vmem_limit_bytes=48 * 1024 * 1024
        ),
        cost_estimate=pl.CostEstimate(
            flops=6_000_000_000, bytes_accessed=2_000_000, transcendentals=0
        ),
    )(*(
        pltpu.with_memory_space_constraint(a, pltpu.HBM)
        for a in (inputs, cotangent, filters, projections)
    ))


def solution(mesh):
    placed = (P("seq", None), P("seq", None), P(), P("filt", None, None))
    return jax.shard_map(
        per_device,
        mesh=mesh,
        in_specs=placed,
        out_specs=(P("seq", "filt"), P("filt", "seq", None)),
        check_vma=False,
    )
```

```python
import functools

import jax
import jax.numpy as jnp
from jax import lax
from jax.experimental import pallas as pl
from jax.experimental.pallas import tpu as pltpu
from jax.sharding import PartitionSpec as P

MESH = pl.DeviceIdType.MESH
F32 = jnp.float32
BF16 = jnp.bfloat16
B = 128
ORDER = (0, 1, -1, 2, -2, 3, -3, 4)


def kernel(
    x_ref, g_ref, f_ref, p_ref, ig_ref, pg_ref,
    taps, fv, gv, xv, hank, gl, g2, acc, corr, xs, xt, pn, pgb, pgr, pgh, pgs, pga, pgo, pgp,
    iga, igb, ra, rb, igt, fa, fb,
    ga_s, ga_r, gr_s, gr_r, gs_s, gs_r, ge_s, ge_r, xa_s, xa_r, xs_s, xs_r, loc,
    pr_s, pr_r, ph_s, ph_r, pa_s, pa_r, pp_s, pp_r, cs_s, cs_r, ip_s, ip_r, iq_s, iq_r,
):
    seq = lax.axis_index("seq")
    filt = lax.axis_index("filt")
    q, z = lax.div(seq, 8), lax.rem(seq, 8)
    xh, core = lax.div(filt, 2), lax.rem(filt, 2)
    x, y = xh * 2 + lax.rem(q, 2), lax.div(q, 2)
    sib = (seq, xh * 2 + 1 - core)
    up = (q * 8 + lax.rem(z + 1, 8), filt)
    down = (q * 8 + lax.rem(z + 7, 8), filt)

    def plane(dx, dq):
        return (lax.rem(q + dq, 8) * 8 + z, lax.rem(xh + dx, 2) * 2 + core)

    def remote(src, dst, send, recv, to):
        return pltpu.make_async_remote_copy(
            src_ref=src, dst_ref=dst, send_sem=send, recv_sem=recv,
            device_id=to, device_id_type=MESH,
        )

    sent = []

    def go(copy):
        copy.start()
        sent.append(copy)

    def settle(count):
        for c in sent[:count]:
            c.wait_send()
        del sent[:count]

    def chip(dx, dy):
        to_x, to_y = lax.rem(x + dx, 4), lax.rem(y + dy, 4)
        return ((to_y * 2 + lax.rem(to_x, 2)) * 8 + z, lax.div(to_x, 2) * 2 + core)

    def near(dz, dq):
        return (lax.rem(q + dq, 8) * 8 + lax.rem(z + dz + 8, 8), filt)

    barrier = pltpu.get_barrier_semaphore()
    partners = (
        [plane(0, r) for r in range(1, 8)]
        + [((y * 2 + side) * 8 + z, (1 - xh) * 2 + core) for side in range(2)]
        + [up, down, sib]
    )
    for to in partners:
        pl.semaphore_signal(barrier, inc=1, device_id=to, device_id_type=MESH)

    rows = pl.ds(pl.multiple_of(core * 64, 64), 64)
    lanes = pl.ds(pl.multiple_of(q * B, B), B)
    own = pl.ds(pl.multiple_of(core * 384, 128), 384)

    def p_slice(k, to, of_core):
        e = pl.ds(pl.multiple_of(to * 512 + of_core * 256, 256), 256)
        return p_ref.at[k, e, lanes]

    def p_place(k, to):
        return pn.at[to, :, pl.ds(pl.multiple_of(core * 384 + k * B, B), B)]

    f_in = pltpu.make_async_copy(f_ref, fv, loc.at[4])
    g_own = pltpu.make_async_copy(g_ref.at[rows, lanes], gl.at[0, core, q], loc.at[6])
    g_in = pltpu.make_async_copy(g_ref.at[rows], gv, loc.at[5])
    x_in = pltpu.make_async_copy(x_ref, xv, loc.at[7])
    p_copies = [
        pltpu.make_async_copy(p_slice(k, to, core), p_place(k, to), loc.at[8 + 2 * k + to])
        for k in range(3)
        for to in range(2)
    ]
    for c in [g_in, g_own, f_in, x_in] + p_copies:
        c.start()
    f_in.wait()
    pick = jnp.where(
        lax.broadcasted_iota(jnp.int32, (8, 12), 1)
        == lax.broadcasted_iota(jnp.int32, (8, 12), 0) + 3 * filt,
        1.0, 0.0,
    ).astype(BF16)
    taps[:, 0:B] = jnp.zeros((8, B), F32)
    taps[:, B:] = jnp.dot(pick, fv[...], preferred_element_type=F32)
    g2[0, 1024:1152, 0:B] = jnp.zeros((B, B), BF16)
    g2[0, 896:1152, B:2 * B] = jnp.zeros((2 * B, B), BF16)

    def build(j, carry):
        for i in range(8):
            upper = lax.broadcasted_iota(jnp.int32, (16, B), 1) >= (
                lax.broadcasted_iota(jnp.int32, (16, B), 0) + 16 * i
            )
            for k in range(3):
                before = None
                for d in range(-1, 8):
                    row = taps[k:k + 1, pl.ds(pl.multiple_of((8 * j + d + 1) * B, B), B)]
                    turned = pltpu.roll(
                        jnp.broadcast_to(row, (16, B)), 16 * i, 1, stride=1, stride_axis=0
                    )
                    if d >= 0:
                        hank[d, k * B + 16 * i:k * B + 16 * i + 16,
                             pl.ds(pl.multiple_of(j * B, B), B)] = jnp.where(
                                 upper, turned, before
                             ).astype(BF16)
                    before = turned
        return carry

    lax.fori_loop(0, 4, build, 0)
    g_in.wait()
    g_own.wait()

    pl.semaphore_wait(barrier, len(partners))

    for n, (dy, side) in enumerate(((2, 1), (2, 0), (1, 1), (3, 1), (1, 0), (3, 0), (0, 1))):
        to_q = lax.rem(y + dy, 4) * 2 + lax.rem(x + side, 2)
        col = pl.ds(pl.multiple_of(to_q * B, B), B)
        go(remote(
            gv.at[:, col], gl.at[0, core, q], ga_s.at[n], ga_r.at[q], (to_q * 8 + z, filt)
        ))
    p_sends = [
        remote(
            p_slice(k, to, 1 - core), p_place(k, to), pp_s.at[2 * k + to], pp_r.at[2 * k + to], sib
        )
        for k in range(3)
        for to in range(2)
    ]
    for c in p_sends:
        go(c)
    lax.fori_loop(4, 8, build, 0)

    x_in.wait()
    for t in range(8):
        flip = xv[:, t * B:(t + 1) * B].T
        for zz in range(8):
            xs[zz, t * 16:(t + 1) * 16, :] = flip[zz * 16:(zz + 1) * 16]
    half = pl.ds(core * 4, 4)
    x_own = pltpu.make_async_copy(xs.at[half], xt.at[half, :, lanes], loc.at[3])
    x_own.start()

    def turn(s):
        return lax.rem(y + (0, 1, 3, 2)[s], 4)

    def sub(slot, s):
        return gl.at[slot, core, pl.ds(turn(s) * 2, 2)]

    def ring_send(step, s, way):
        here = -step % 8 if way == 0 else step
        there = (-step - 1) % 8 if way == 0 else step + 1
        return remote(
            sub(here, s), sub(there, s),
            gr_s.at[way, step, s], gr_r.at[way, step, s], up if way == 0 else down,
        )

    def hand_over(slot):
        mine = gl.at[slot, core]
        return remote(mine, mine, gs_s.at[slot], gs_r.at[slot], sib)

    def handed(slot):
        other = gl.at[slot, 1 - core]
        return remote(other, other, gs_s.at[slot], gs_r.at[slot], sib)

    def landed(from_q):
        here = gl.at[0, core, from_q]
        remote(here, here, ga_s.at[0], ga_r.at[from_q], up).wait_recv()

    landed(lax.div(q, 2) * 2 + lax.rem(q + 1, 2))
    for s in range(4):
        if s:
            landed(turn(s) * 2)
            landed(turn(s) * 2 + 1)
        for way in range(2):
            go(ring_send(0, s, way))
    go(hand_over(0))

    x_sends = []
    for r in range(1, 8):
        x_sends.append(
            remote(xs.at[half], xt.at[half, :, lanes], xa_s.at[r], xa_r.at[r], plane(0, r))
        )
        go(x_sends[-1])

    corr_sends = []

    def conv(o):
        slot = o % 8
        if o == 4:
            for s in range(4):
                other = gl.at[4, 1 - core, pl.ds(turn(s) * 2, 2)]
                remote(other, other, ge_s.at[s], ge_r.at[s], sib).wait_recv()
        else:
            handed(slot).wait_recv()
        buf = g2.at[0]
        for m in range(8):
            for h in range(2):
                piece = gl[slot, h, m]
                buf[m * B + h * 64:m * B + h * 64 + 64, 0:B] = piece
                if m > 0:
                    buf[(m - 1) * B + h * 64:(m - 1) * B + h * 64 + 64, B:2 * B] = piece
        wrap = jnp.where(lax.rem(z + o + 8, 8) < z, 1, 0)
        for p in range(4):
            depth = B * (8 - 2 * p)
            start = pl.multiple_of(wrap * B + 2 * p * B, B)
            term = jnp.dot(
                hank[slot, :, 0:depth], buf[pl.ds(start, depth), :],
                preferred_element_type=F32,
            )
            if o == 0:
                acc[p] = term
            elif o != 4:
                acc[p] += term
            else:
                done = (acc[p] + term).astype(BF16)
                for e in range(2):
                    for k in range(3):
                        corr[
                            (2 * p + e) * B:(2 * p + e + 1) * B,
                            pl.ds(pl.multiple_of(core * 384 + k * B, B), B),
                        ] = done[k * B:(k + 1) * B, e * B:(e + 1) * B]
                mine = corr.at[pl.ds(p * 256, 256), own]
                corr_sends.append(remote(mine, mine, cs_s.at[p], cs_r.at[p], sib))
                go(corr_sends[-1])

    conv(0)
    for step in range(1, 4):
        for s in range(4):
            for way in range(2):
                ring_send(step - 1, s, way).wait_recv()
                if step < 3 or s // 2 == way:
                    go(ring_send(step, s, way))
        go(hand_over(-step % 8))
        go(hand_over(step))
        if step > 1:
            conv(step - 1)
            conv(1 - step)
        if step == 3:
            x_own.wait()
            for c in x_sends:
                c.wait_recv()
            x_hand = remote(xt.at[half], xt.at[half], xs_s, xs_r, sib)
            go(x_hand)
    early = len(sent)
    conv(3)
    for s in range(4):
        ring_send(3, s, s // 2).wait_recv()
        mine = sub(4, s)
        go(remote(mine, mine, ge_s.at[s], ge_r.at[s], sib))
    conv(-3)
    conv(4)

    half_o = pl.ds((1 - core) * 4, 4)
    remote(xt.at[half_o], xt.at[half_o], xs_s, xs_r, sib).wait_recv()

    def at(o):
        return lax.rem(z + o + 8, 8)

    def products(*offsets):
        for o in offsets:
            part = jnp.dot(xt[at(o)], corr[:, own], preferred_element_type=F32).astype(BF16)
            for k in range(3):
                if o == 0:
                    pgo[:, k] = part[:, k * B:(k + 1) * B].reshape(8, 16, B)
                else:
                    pgb[at(o), k] = part[:, k * B:(k + 1) * B]

    def sum_send(step, k, way):
        src = pgb.at[at(3 if way == 0 else -3), k] if step == 0 else pgs.at[way, k]
        return remote(
            src, pgr.at[way, step, k], pr_s.at[way, step, k], pr_r.at[way, step, k],
            up if way == 0 else down,
        )

    def far_send(k, way):
        return remote(
            pgb.at[at(4), k, pl.ds(way * 64, 64)], pgh.at[way, k], ph_s.at[way, k],
            ph_r.at[way, k], near(2 if way == 0 else -2, 0),
        )

    def sum_step(step, k, way):
        o = 3 - step if way == 0 else step - 3
        sum_send(step - 1, k, way).wait_recv()
        total = pgr[way, step - 1, k].astype(F32) + pgb[at(o), k].astype(F32)
        if step == 1:
            far_send(k, way).wait_recv()
            far = pgh[way, k].astype(F32)
            pgs[way, k, way * 64:way * 64 + 64] = (
                total[way * 64:way * 64 + 64] + far
            ).astype(BF16)
            pgs[way, k, 64 - way * 64:128 - way * 64] = total[
                64 - way * 64:128 - way * 64
            ].astype(BF16)
            go(sum_send(step, k, way))
        else:
            pga[way, :, k] = total.astype(BF16).reshape(8, 16, B)
        if step == 2 and k == 2:
            for r in range(8):
                go(remote(
                    pga.at[way, lax.rem(q + r, 8)], pgp.at[way + 1, q],
                    pa_s.at[way + 1, r], pa_r.at[way + 1, q], near(1 if way == 0 else -1, r),
                ))

    products(4)
    for k in range(3):
        for way in range(2):
            go(far_send(k, way))
    products(3, -3)
    for k in range(3):
        for way in range(2):
            go(sum_send(0, k, way))

    for c in p_copies:
        c.wait()
    for c in p_sends:
        c.wait_recv()
    for c in corr_sends:
        c.wait_recv()
    ig_sends = []
    for dy in (2, 1, 3, 0):
        pair = lax.rem(y + dy, 4)
        rows_of = corr[pl.ds(pl.multiple_of(pair * 256, 256), 256), :]
        for to in range(2):
            part = lax.dot_general(
                rows_of, pn[to], (((1,), (1,)), ((), ())), preferred_element_type=F32
            ).astype(BF16)
            for side in range(2):
                iga[2 * to + side, pair] = part[side * B:(side + 1) * B, 0:B]
                igb[pair, 2 * to + side] = part[side * B:(side + 1) * B, B:2 * B]
        if dy:
            ig_sends.append(remote(
                igb.at[pair], rb.at[dy], ip_s.at[1, dy], ip_r.at[1, dy], chip(0, dy)
            ))
            go(ig_sends[-1])
    for dx in (2, 1, 3):
        ig_sends.append(remote(
            iga.at[lax.rem(x + dx, 4)], ra.at[dx], ip_s.at[0, dx], ip_r.at[0, dx], chip(dx, 0)
        ))
        go(ig_sends[-1])

    products(2, -2)
    for k in range(3):
        for way in range(2):
            sum_step(1, k, way)
    settle(early)
    products(1, -1, 0)
    pg_sends = []
    for r in range(1, 8):
        pg_sends.append(
            remote(
                pgo.at[lax.rem(q + r, 8)], pgp.at[0, q], pa_s.at[0, r], pa_r.at[0, r],
                plane(0, r),
            )
        )
        go(pg_sends[-1])
    pgp[0, q] = pgo[q]
    for k in range(3):
        for way in range(2):
            sum_step(2, k, way)

    middle = len(sent) - 23
    for c in ig_sends:
        c.wait_recv()
    ig_last = []
    for d in (2, 1, 3):
        for mine, got, last, n in ((iga.at[x], ra, fa, 0), (igb.at[y], rb, fb, 1)):
            there = lax.rem((y if n == 0 else x) + d, 4)
            total = mine[there].astype(F32)
            for e in range(1, 4):
                total = total + got[e, there].astype(F32)
            out = igt.at[n, d]
            out[...] = total.astype(BF16)
            ig_last.append(remote(
                out, last.at[d], iq_s.at[n, d], iq_r.at[n, d],
                chip(0, d) if n == 0 else chip(d, 0),
            ))
            go(ig_last[-1])

    settle(middle)
    halves = []
    for mine, got, here in ((iga.at[x], ra, y), (igb.at[y], rb, x)):
        total = mine[here].astype(F32)
        for e in range(1, 4):
            total = total + got[e, here].astype(F32)
        halves.append(total)
    for c in ig_last:
        c.wait_recv()
    for n, last in ((0, fa), (1, fb)):
        total = halves[n]
        for e in range(1, 4):
            total = total + last[e].astype(F32)
        ig_ref[:, n * B:(n + 1) * B] = total.astype(BF16)

    for c in pg_sends:
        c.wait_recv()
    for s in range(8):
        for d in (1, 2):
            here = pgp.at[d, s]
            remote(here, here, pa_s.at[d, 0], pa_r.at[d, s], up).wait_recv()
        total = (
            pgp[0, s].astype(F32) + pgp[1, s].astype(F32) + pgp[2, s].astype(F32)
        ) * (8192.0 ** -0.5)
        pg_ref[:, :, s * B:(s + 1) * B] = total.astype(BF16)
    settle(len(sent))


def per_device(inputs, cotangent, filters, projections):
    vmem = pl.BlockSpec(memory_space=pltpu.VMEM)
    dma = pltpu.SemaphoreType.DMA
    return pl.pallas_call(
        kernel,
        out_shape=(
            jax.ShapeDtypeStruct((B, 256), BF16),
            jax.ShapeDtypeStruct((3, 16, 1024), BF16),
        ),
        in_specs=[pl.BlockSpec(memory_space=pl.ANY)] * 4,
        out_specs=(vmem, vmem),
        scratch_shapes=[
            pltpu.VMEM((8, 8192 + B), F32),
            pltpu.VMEM((12, 8192), BF16),
            pltpu.VMEM((64, 1024), BF16),
            pltpu.VMEM((B, 1024), BF16),
            pltpu.VMEM((8, 384, 1024), BF16),
            pltpu.VMEM((8, 2, 8, 64, B), BF16),
            pltpu.VMEM((1, 1152, 256), BF16),
            pltpu.VMEM((4, 384, 256), F32),
            pltpu.VMEM((1024, 768), BF16),
            pltpu.VMEM((8, B, B), BF16),
            pltpu.VMEM((8, B, 1024), BF16),
            pltpu.VMEM((2, 256, 768), BF16),
            pltpu.VMEM((8, 3, B, B), BF16),
            pltpu.VMEM((2, 2, 3, B, B), BF16),
            pltpu.VMEM((2, 3, 64, B), BF16),
            pltpu.VMEM((2, 3, B, B), BF16),
            pltpu.VMEM((2, 8, 3, 16, B), BF16),
            pltpu.VMEM((8, 3, 16, B), BF16),
            pltpu.VMEM((3, 8, 3, 16, B), BF16),
            pltpu.VMEM((4, 4, B, B), BF16),
            pltpu.VMEM((4, 4, B, B), BF16),
            pltpu.VMEM((4, 4, B, B), BF16),
            pltpu.VMEM((4, 4, B, B), BF16),
            pltpu.VMEM((2, 4, B, B), BF16),
            pltpu.VMEM((4, B, B), BF16),
            pltpu.VMEM((4, B, B), BF16),
            dma((8,)), dma((8,)),
            dma((2, 4, 4)), dma((2, 4, 4)),
            dma((8,)), dma((8,)),
            dma((4,)), dma((4,)),
            dma((8,)), dma((8,)),
            dma, dma,
            dma((14,)),
            dma((2, 2, 3)), dma((2, 2, 3)),
            dma((2, 3)), dma((2, 3)),
            dma((3, 8)), dma((3, 8)),
            dma((6,)), dma((6,)),
            dma((4,)), dma((4,)),
            dma((2, 4)), dma((2, 4)),
            dma((2, 4)), dma((2, 4)),
        ],
        compiler_params=pltpu.CompilerParams(
            collective_id=0, has_side_effects=True, vmem_limit_bytes=48 * 1024 * 1024
        ),
        cost_estimate=pl.CostEstimate(
            flops=6_000_000_000, bytes_accessed=2_000_000, transcendentals=0
        ),
    )(*(
        pltpu.with_memory_space_constraint(a, pltpu.HBM)
        for a in (inputs, cotangent, filters, projections)
    ))


def solution(mesh):
    placed = (P("seq", None), P("seq", None), P(), P("filt", None, None))
    return jax.shard_map(
        per_device,
        mesh=mesh,
        in_specs=placed,
        out_specs=(P("seq", "filt"), P("filt", "seq", None)),
        check_vma=False,
    )
```

```python
import functools

import jax
import jax.numpy as jnp
from jax import lax
from jax.experimental import pallas as pl
from jax.experimental.pallas import tpu as pltpu
from jax.sharding import PartitionSpec as P

MESH = pl.DeviceIdType.MESH
F32 = jnp.float32
BF16 = jnp.bfloat16
B = 128
ORDER = (0, 1, -1, 2, -2, 3, -3, 4)


def kernel(
    x_ref, g_ref, f_ref, p_ref, ig_ref, pg_ref,
    taps, fv, gv, xv, hank, gl, g2, acc, corr, xs, xt, pn, pgb, pgr, pgh, pgs, pga, pgo, pgp,
    iga, igb, ra, rb, igt, fa, fb,
    ga_s, ga_r, gr_s, gr_r, gs_s, gs_r, ge_s, ge_r, xa_s, xa_r, xs_s, xs_r, loc,
    pr_s, pr_r, ph_s, ph_r, pa_s, pa_r, pp_s, pp_r, cs_s, cs_r, ip_s, ip_r, iq_s, iq_r,
):
    seq = lax.axis_index("seq")
    filt = lax.axis_index("filt")
    q, z = lax.div(seq, 8), lax.rem(seq, 8)
    xh, core = lax.div(filt, 2), lax.rem(filt, 2)
    x, y = xh * 2 + lax.rem(q, 2), lax.div(q, 2)
    sib = (seq, xh * 2 + 1 - core)
    up = (q * 8 + lax.rem(z + 1, 8), filt)
    down = (q * 8 + lax.rem(z + 7, 8), filt)

    def plane(dx, dq):
        return (lax.rem(q + dq, 8) * 8 + z, lax.rem(xh + dx, 2) * 2 + core)

    def remote(src, dst, send, recv, to):
        return pltpu.make_async_remote_copy(
            src_ref=src, dst_ref=dst, send_sem=send, recv_sem=recv,
            device_id=to, device_id_type=MESH,
        )

    sent = []

    def go(copy):
        copy.start()
        sent.append(copy)

    def settle(count):
        for c in sent[:count]:
            c.wait_send()
        del sent[:count]

    def chip(dx, dy):
        to_x, to_y = lax.rem(x + dx, 4), lax.rem(y + dy, 4)
        return ((to_y * 2 + lax.rem(to_x, 2)) * 8 + z, lax.div(to_x, 2) * 2 + core)

    def near(dz, dq):
        return (lax.rem(q + dq, 8) * 8 + lax.rem(z + dz + 8, 8), filt)

    barrier = pltpu.get_barrier_semaphore()
    partners = (
        [plane(0, r) for r in range(1, 8)]
        + [((y * 2 + side) * 8 + z, (1 - xh) * 2 + core) for side in range(2)]
        + [up, down, sib]
    )
    for to in partners:
        pl.semaphore_signal(barrier, inc=1, device_id=to, device_id_type=MESH)

    rows = pl.ds(pl.multiple_of(core * 64, 64), 64)
    lanes = pl.ds(pl.multiple_of(q * B, B), B)
    own = pl.ds(pl.multiple_of(core * 384, 128), 384)

    def p_slice(k, to, of_core):
        e = pl.ds(pl.multiple_of(to * 512 + of_core * 256, 256), 256)
        return p_ref.at[k, e, lanes]

    def p_place(k, to):
        return pn.at[to, :, pl.ds(pl.multiple_of(core * 384 + k * B, B), B)]

    f_in = pltpu.make_async_copy(f_ref, fv, loc.at[4])
    g_own = pltpu.make_async_copy(g_ref.at[rows, lanes], gl.at[0, core, q], loc.at[6])
    g_in = pltpu.make_async_copy(g_ref.at[rows], gv, loc.at[5])
    x_in = pltpu.make_async_copy(x_ref, xv, loc.at[7])
    p_copies = [
        pltpu.make_async_copy(p_slice(k, to, core), p_place(k, to), loc.at[8 + 2 * k + to])
        for k in range(3)
        for to in range(2)
    ]
    for c in [g_in, g_own, f_in, x_in] + p_copies:
        c.start()
    f_in.wait()
    pick = jnp.where(
        lax.broadcasted_iota(jnp.int32, (8, 12), 1)
        == lax.broadcasted_iota(jnp.int32, (8, 12), 0) + 3 * filt,
        1.0, 0.0,
    ).astype(BF16)
    taps[:, 0:B] = jnp.zeros((8, B), F32)
    taps[:, B:] = jnp.dot(pick, fv[...], preferred_element_type=F32)
    g2[0, 1024:1152, 0:B] = jnp.zeros((B, B), BF16)
    g2[0, 896:1152, B:2 * B] = jnp.zeros((2 * B, B), BF16)

    def build(j, carry):
        for i in range(8):
            upper = lax.broadcasted_iota(jnp.int32, (16, B), 1) >= (
                lax.broadcasted_iota(jnp.int32, (16, B), 0) + 16 * i
            )
            for k in range(3):
                before = None
                for d in range(-1, 8):
                    row = taps[k:k + 1, pl.ds(pl.multiple_of((8 * j + d + 1) * B, B), B)]
                    turned = pltpu.roll(
                        jnp.broadcast_to(row, (16, B)), 16 * i, 1, stride=1, stride_axis=0
                    )
                    if d >= 0:
                        hank[d, k * B + 16 * i:k * B + 16 * i + 16,
                             pl.ds(pl.multiple_of(j * B, B), B)] = jnp.where(
                                 upper, turned, before
                             ).astype(BF16)
                    before = turned
        return carry

    lax.fori_loop(0, 4, build, 0)
    g_in.wait()
    g_own.wait()

    pl.semaphore_wait(barrier, len(partners))

    for n, (dy, side) in enumerate(((2, 1), (2, 0), (1, 1), (3, 1), (1, 0), (3, 0), (0, 1))):
        to_q = lax.rem(y + dy, 4) * 2 + lax.rem(x + side, 2)
        col = pl.ds(pl.multiple_of(to_q * B, B), B)
        go(remote(
            gv.at[:, col], gl.at[0, core, q], ga_s.at[n], ga_r.at[q], (to_q * 8 + z, filt)
        ))
    p_sends = [
        remote(
            p_slice(k, to, 1 - core), p_place(k, to), pp_s.at[2 * k + to], pp_r.at[2 * k + to], sib
        )
        for k in range(3)
        for to in range(2)
    ]
    for c in p_sends:
        go(c)
    lax.fori_loop(4, 8, build, 0)

    x_in.wait()
    for t in range(8):
        flip = xv[:, t * B:(t + 1) * B].T
        for zz in range(8):
            xs[zz, t * 16:(t + 1) * 16, :] = flip[zz * 16:(zz + 1) * 16]
    half = pl.ds(core * 4, 4)
    x_own = pltpu.make_async_copy(xs.at[half], xt.at[half, :, lanes], loc.at[3])
    x_own.start()

    def turn(s):
        return lax.rem(y + (0, 1, 3, 2)[s], 4)

    def sub(slot, s):
        return gl.at[slot, core, pl.ds(turn(s) * 2, 2)]

    def ring_send(step, s, way):
        here = -step % 8 if way == 0 else step
        there = (-step - 1) % 8 if way == 0 else step + 1
        return remote(
            sub(here, s), sub(there, s),
            gr_s.at[way, step, s], gr_r.at[way, step, s], up if way == 0 else down,
        )

    def hand_over(slot):
        mine = gl.at[slot, core]
        return remote(mine, mine, gs_s.at[slot], gs_r.at[slot], sib)

    def handed(slot):
        other = gl.at[slot, 1 - core]
        return remote(other, other, gs_s.at[slot], gs_r.at[slot], sib)

    def landed(from_q):
        here = gl.at[0, core, from_q]
        remote(here, here, ga_s.at[0], ga_r.at[from_q], up).wait_recv()

    landed(lax.div(q, 2) * 2 + lax.rem(q + 1, 2))
    for s in range(4):
        if s:
            landed(turn(s) * 2)
            landed(turn(s) * 2 + 1)
        for way in range(2):
            go(ring_send(0, s, way))
    go(hand_over(0))

    x_sends = []
    for r in range(1, 8):
        x_sends.append(
            remote(xs.at[half], xt.at[half, :, lanes], xa_s.at[r], xa_r.at[r], plane(0, r))
        )
        go(x_sends[-1])

    corr_sends = []

    def conv(o):
        slot = o % 8
        if o == 4:
            for s in range(4):
                other = gl.at[4, 1 - core, pl.ds(turn(s) * 2, 2)]
                remote(other, other, ge_s.at[s], ge_r.at[s], sib).wait_recv()
        else:
            handed(slot).wait_recv()
        buf = g2.at[0]
        for m in range(8):
            for h in range(2):
                piece = gl[slot, h, m]
                buf[m * B + h * 64:m * B + h * 64 + 64, 0:B] = piece
                if m > 0:
                    buf[(m - 1) * B + h * 64:(m - 1) * B + h * 64 + 64, B:2 * B] = piece
        wrap = jnp.where(lax.rem(z + o + 8, 8) < z, 1, 0)
        for p in range(4):
            depth = B * (8 - 2 * p)
            start = pl.multiple_of(wrap * B + 2 * p * B, B)
            term = jnp.dot(
                hank[slot, :, 0:depth], buf[pl.ds(start, depth), :],
                preferred_element_type=F32,
            )
            if o == 0:
                acc[p] = term
            elif o != 4:
                acc[p] += term
            else:
                done = (acc[p] + term).astype(BF16)
                for e in range(2):
                    for k in range(3):
                        corr[
                            (2 * p + e) * B:(2 * p + e + 1) * B,
                            pl.ds(pl.multiple_of(core * 384 + k * B, B), B),
                        ] = done[k * B:(k + 1) * B, e * B:(e + 1) * B]
                mine = corr.at[pl.ds(p * 256, 256), own]
                corr_sends.append(remote(mine, mine, cs_s.at[p], cs_r.at[p], sib))
                go(corr_sends[-1])

    conv(0)
    for step in range(1, 4):
        for s in range(4):
            for way in range(2):
                ring_send(step - 1, s, way).wait_recv()
                if step < 3 or s // 2 == way:
                    go(ring_send(step, s, way))
        go(hand_over(-step % 8))
        go(hand_over(step))
        if step > 1:
            conv(step - 1)
            conv(1 - step)
        if step == 3:
            x_own.wait()
            for c in x_sends:
                c.wait_recv()
            x_hand = remote(xt.at[half], xt.at[half], xs_s, xs_r, sib)
            go(x_hand)
    early = len(sent)
    conv(3)
    for s in range(4):
        ring_send(3, s, s // 2).wait_recv()
        mine = sub(4, s)
        go(remote(mine, mine, ge_s.at[s], ge_r.at[s], sib))
    conv(-3)
    conv(4)

    half_o = pl.ds((1 - core) * 4, 4)
    remote(xt.at[half_o], xt.at[half_o], xs_s, xs_r, sib).wait_recv()

    def at(o):
        return lax.rem(z + o + 8, 8)

    def products(*offsets):
        for o in offsets:
            part = jnp.dot(xt[at(o)], corr[:, own], preferred_element_type=F32).astype(BF16)
            for k in range(3):
                if o == 0:
                    pgo[:, k] = part[:, k * B:(k + 1) * B].reshape(8, 16, B)
                else:
                    pgb[at(o), k] = part[:, k * B:(k + 1) * B]

    def sum_send(step, k, way):
        src = pgb.at[at(3 if way == 0 else -3), k] if step == 0 else pgs.at[way, k]
        return remote(
            src, pgr.at[way, step, k], pr_s.at[way, step, k], pr_r.at[way, step, k],
            up if way == 0 else down,
        )

    def far_send(k, way):
        return remote(
            pgb.at[at(4), k, pl.ds(way * 64, 64)], pgh.at[way, k], ph_s.at[way, k],
            ph_r.at[way, k], near(2 if way == 0 else -2, 0),
        )

    def sum_step(step, k, way):
        o = 3 - step if way == 0 else step - 3
        sum_send(step - 1, k, way).wait_recv()
        total = pgr[way, step - 1, k].astype(F32) + pgb[at(o), k].astype(F32)
        if step == 1:
            far_send(k, way).wait_recv()
            far = pgh[way, k].astype(F32)
            pgs[way, k, way * 64:way * 64 + 64] = (
                total[way * 64:way * 64 + 64] + far
            ).astype(BF16)
            pgs[way, k, 64 - way * 64:128 - way * 64] = total[
                64 - way * 64:128 - way * 64
            ].astype(BF16)
            go(sum_send(step, k, way))
        else:
            pga[way, :, k] = total.astype(BF16).reshape(8, 16, B)
        if step == 2 and k == 2:
            for r in range(8):
                go(remote(
                    pga.at[way, lax.rem(q + r, 8)], pgp.at[way + 1, q],
                    pa_s.at[way + 1, r], pa_r.at[way + 1, q], near(1 if way == 0 else -1, r),
                ))

    products(3, -3)
    for way in range(2):
        go(sum_send(0, 0, way))
    products(4)
    for k in range(3):
        for way in range(2):
            go(far_send(k, way))
            if k:
                go(sum_send(0, k, way))

    for c in p_copies:
        c.wait()
    for c in p_sends:
        c.wait_recv()
    for c in corr_sends:
        c.wait_recv()
    ig_sends = []
    for dy in (2, 1, 3, 0):
        pair = lax.rem(y + dy, 4)
        rows_of = corr[pl.ds(pl.multiple_of(pair * 256, 256), 256), :]
        for to in range(2):
            part = lax.dot_general(
                rows_of, pn[to], (((1,), (1,)), ((), ())), preferred_element_type=F32
            ).astype(BF16)
            for side in range(2):
                iga[2 * to + side, pair] = part[side * B:(side + 1) * B, 0:B]
                igb[pair, 2 * to + side] = part[side * B:(side + 1) * B, B:2 * B]
        if dy:
            ig_sends.append(remote(
                igb.at[pair], rb.at[dy], ip_s.at[1, dy], ip_r.at[1, dy], chip(0, dy)
            ))
            go(ig_sends[-1])
    for dx in (2, 1, 3):
        ig_sends.append(remote(
            iga.at[lax.rem(x + dx, 4)], ra.at[dx], ip_s.at[0, dx], ip_r.at[0, dx], chip(dx, 0)
        ))
        go(ig_sends[-1])

    products(2, -2)
    for k in range(3):
        for way in range(2):
            sum_step(1, k, way)
    settle(early)
    products(1, -1, 0)
    pg_sends = []
    for r in range(1, 8):
        pg_sends.append(
            remote(
                pgo.at[lax.rem(q + r, 8)], pgp.at[0, q], pa_s.at[0, r], pa_r.at[0, r],
                plane(0, r),
            )
        )
        go(pg_sends[-1])
    pgp[0, q] = pgo[q]
    for k in range(3):
        for way in range(2):
            sum_step(2, k, way)

    middle = len(sent) - 23
    for c in ig_sends:
        c.wait_recv()
    ig_last = []
    for d in (2, 1, 3):
        for mine, got, last, n in ((iga.at[x], ra, fa, 0), (igb.at[y], rb, fb, 1)):
            there = lax.rem((y if n == 0 else x) + d, 4)
            total = mine[there].astype(F32)
            for e in range(1, 4):
                total = total + got[e, there].astype(F32)
            out = igt.at[n, d]
            out[...] = total.astype(BF16)
            ig_last.append(remote(
                out, last.at[d], iq_s.at[n, d], iq_r.at[n, d],
                chip(0, d) if n == 0 else chip(d, 0),
            ))
            go(ig_last[-1])

    settle(middle)
    halves = []
    for mine, got, here in ((iga.at[x], ra, y), (igb.at[y], rb, x)):
        total = mine[here].astype(F32)
        for e in range(1, 4):
            total = total + got[e, here].astype(F32)
        halves.append(total)
    for c in ig_last:
        c.wait_recv()
    for n, last in ((0, fa), (1, fb)):
        total = halves[n]
        for e in range(1, 4):
            total = total + last[e].astype(F32)
        ig_ref[:, n * B:(n + 1) * B] = total.astype(BF16)

    for c in pg_sends:
        c.wait_recv()
    for s in range(8):
        for d in (1, 2):
            here = pgp.at[d, s]
            remote(here, here, pa_s.at[d, 0], pa_r.at[d, s], up).wait_recv()
        total = (
            pgp[0, s].astype(F32) + pgp[1, s].astype(F32) + pgp[2, s].astype(F32)
        ) * (8192.0 ** -0.5)
        pg_ref[:, :, s * B:(s + 1) * B] = total.astype(BF16)
    settle(len(sent))


def per_device(inputs, cotangent, filters, projections):
    vmem = pl.BlockSpec(memory_space=pltpu.VMEM)
    dma = pltpu.SemaphoreType.DMA
    return pl.pallas_call(
        kernel,
        out_shape=(
            jax.ShapeDtypeStruct((B, 256), BF16),
            jax.ShapeDtypeStruct((3, 16, 1024), BF16),
        ),
        in_specs=[pl.BlockSpec(memory_space=pl.ANY)] * 4,
        out_specs=(vmem, vmem),
        scratch_shapes=[
            pltpu.VMEM((8, 8192 + B), F32),
            pltpu.VMEM((12, 8192), BF16),
            pltpu.VMEM((64, 1024), BF16),
            pltpu.VMEM((B, 1024), BF16),
            pltpu.VMEM((8, 384, 1024), BF16),
            pltpu.VMEM((8, 2, 8, 64, B), BF16),
            pltpu.VMEM((1, 1152, 256), BF16),
            pltpu.VMEM((4, 384, 256), F32),
            pltpu.VMEM((1024, 768), BF16),
            pltpu.VMEM((8, B, B), BF16),
            pltpu.VMEM((8, B, 1024), BF16),
            pltpu.VMEM((2, 256, 768), BF16),
            pltpu.VMEM((8, 3, B, B), BF16),
            pltpu.VMEM((2, 2, 3, B, B), BF16),
            pltpu.VMEM((2, 3, 64, B), BF16),
            pltpu.VMEM((2, 3, B, B), BF16),
            pltpu.VMEM((2, 8, 3, 16, B), BF16),
            pltpu.VMEM((8, 3, 16, B), BF16),
            pltpu.VMEM((3, 8, 3, 16, B), BF16),
            pltpu.VMEM((4, 4, B, B), BF16),
            pltpu.VMEM((4, 4, B, B), BF16),
            pltpu.VMEM((4, 4, B, B), BF16),
            pltpu.VMEM((4, 4, B, B), BF16),
            pltpu.VMEM((2, 4, B, B), BF16),
            pltpu.VMEM((4, B, B), BF16),
            pltpu.VMEM((4, B, B), BF16),
            dma((8,)), dma((8,)),
            dma((2, 4, 4)), dma((2, 4, 4)),
            dma((8,)), dma((8,)),
            dma((4,)), dma((4,)),
            dma((8,)), dma((8,)),
            dma, dma,
            dma((14,)),
            dma((2, 2, 3)), dma((2, 2, 3)),
            dma((2, 3)), dma((2, 3)),
            dma((3, 8)), dma((3, 8)),
            dma((6,)), dma((6,)),
            dma((4,)), dma((4,)),
            dma((2, 4)), dma((2, 4)),
            dma((2, 4)), dma((2, 4)),
        ],
        compiler_params=pltpu.CompilerParams(
            collective_id=0, has_side_effects=True, vmem_limit_bytes=48 * 1024 * 1024
        ),
        cost_estimate=pl.CostEstimate(
            flops=6_000_000_000, bytes_accessed=2_000_000, transcendentals=0
        ),
    )(*(
        pltpu.with_memory_space_constraint(a, pltpu.HBM)
        for a in (inputs, cotangent, filters, projections)
    ))


def solution(mesh):
    placed = (P("seq", None), P("seq", None), P(), P("filt", None, None))
    return jax.shard_map(
        per_device,
        mesh=mesh,
        in_specs=placed,
        out_specs=(P("seq", "filt"), P("filt", "seq", None)),
        check_vma=False,
    )
```
